32 devices in a mesh: gx: 16 (over z, x, core), gz: 2 (over y).
Axes of the slice: x: 2, y: 2, z: 4, core: 2. Of those that a mesh axis runs over, the one named last changes fastest.
Arguments:
- u_vel: bfloat16 [512, 384, 768], P('gx', 'gz'), may hold values from -6 to 6
- v_vel: bfloat16 [512, 384, 768], P('gx', 'gz'), may hold values from -6 to 6
- w_vel: bfloat16 [512, 384, 768], P('gx', 'gz'), may hold values from -6 to 6
Outputs:
- pressure: float32 [512, 384, 768], P('gx', 'gz')
- u_new: float32 [512, 384, 768], P('gx', 'gz')
- v_new: float32 [512, 384, 768], P('gx', 'gz')
- w_new: float32 [512, 384, 768], P('gx', 'gz')
The draws below stay inside these ranges and needn't reach their ends.
All inputs are finite; a program needn't handle non-finite values.
Results may differ from the reference program's by a relative error of at most 0.002.
Values may be sent and summed in bfloat16 or wider, within the bound.
No kernel may reach another device: no remote copies, remote signals or barrier semaphores. Data moves between devices by JAX's collectives and lax.ppermute only.
A program may use at most 192 MiB of HBM per device.

```python
import math
import jax
import jax.numpy as jnp
from jax import lax

NX = 512
NY = 768
NZ = 384


def level_of(stream_key, dims, shards, smallest, largest):
    level, own = 1.0, jax.random.fold_in(stream_key, 6)
    for axis_at, blocks in shards:
        heights = jnp.exp(jax.random.uniform(jax.random.fold_in(own, axis_at), (blocks,), jnp.float32, smallest / len(shards), largest / len(shards)))
        level = level * jnp.repeat(heights, dims[axis_at] // blocks).reshape([-1 if axis == axis_at else 1 for axis in range(len(dims))])
    return level


def centred(stream_key, extent, scale, most, shards=(), kind=jnp.bfloat16):
    factor_of = level_of(stream_key, extent, shards, -0.22, 0.18) if shards else 1.0
    result = jax.random.normal(stream_key, extent, jnp.float32) * scale * factor_of
    return jnp.minimum(jnp.maximum(result, -most), most).astype(kind)


def setup_inputs(seed: int = 0) -> dict:
    streams_of = jax.random.split(jax.random.key(seed), 4)
    return {
        "u_vel": centred(streams_of[0], (NX, NZ, NY), 1.0, 6.0, ((0, 16), (1, 2))),
        "v_vel": centred(streams_of[1], (NX, NZ, NY), 1.0, 6.0, ((0, 16), (1, 2))),
        "w_vel": centred(streams_of[2], (NX, NZ, NY), 1.0, 6.0, ((0, 16), (1, 2))),
    }


def hartley_table(count):
    index = jnp.arange(count, dtype=jnp.int32)
    product = index[:, None] * index[None, :] % count
    angle = product.astype(jnp.float32) * (2.0 * math.pi / count)
    return jnp.cos(angle) + jnp.sin(angle)

def sine_table(count):
    index = jnp.arange(1, count + 1, dtype=jnp.int32)
    product = index[:, None] * index[None, :] % (2 * (count + 1))
    angle = product.astype(jnp.float32) * (math.pi / (count + 1))
    return math.sqrt(2.0 / (count + 1)) * jnp.sin(angle)

def periodic_eigen(count):
    index = jnp.arange(count, dtype=jnp.int32).astype(jnp.float32)
    return -4.0 * jnp.sin(index * (math.pi / count)) ** 2

def wall_eigen(count):
    index = jnp.arange(1, count + 1, dtype=jnp.int32).astype(jnp.float32)
    return -4.0 * jnp.sin(index * (math.pi / (2 * count + 2))) ** 2

def wall_slope(field):
    padded = jnp.pad(field, ((0, 0), (0, 0), (1, 1)))
    return 0.5 * (padded[:, :, 2:] - padded[:, :, :-2])

def reference(u_vel, v_vel, w_vel):
    hi = lax.Precision.HIGHEST
    uf = u_vel.astype(jnp.float32)
    vf = v_vel.astype(jnp.float32)
    wf = w_vel.astype(jnp.float32)
    div = 0.5 * (jnp.roll(uf, -1, 0) - jnp.roll(uf, 1, 0))
    div = div + 0.5 * (jnp.roll(wf, -1, 1) - jnp.roll(wf, 1, 1))
    div = div + wall_slope(vf)
    sine = sine_table(NY)
    hx = hartley_table(NX)
    hz = hartley_table(NZ)
    spec = jnp.einsum('xzy,ym->xzm', div, sine, precision=hi)
    spec = jnp.einsum('kx,xzm->kzm', hx, spec, precision=hi)
    spec = jnp.einsum('xzm,zq->xqm', spec, hz, precision=hi)
    lam = periodic_eigen(NX)[:, None, None] + periodic_eigen(NZ)[None, :, None] + wall_eigen(NY)[None, None, :]
    spec = spec / (lam * float(NX * NZ))
    spec = jnp.einsum('xqm,zq->xzm', spec, hz, precision=hi)
    spec = jnp.einsum('kx,xzm->kzm', hx, spec, precision=hi)
    pressure = jnp.einsum('xzm,my->xzy', spec, sine, precision=hi)
    slope_x = 0.5 * (jnp.roll(pressure, -1, 0) - jnp.roll(pressure, 1, 0))
    slope_z = 0.5 * (jnp.roll(pressure, -1, 1) - jnp.roll(pressure, 1, 1))
    u_new = uf - slope_x
    v_new = vf - wall_slope(pressure)
    w_new = wf - slope_z
    return (pressure, u_new, v_new, w_new)
```

```python
import functools
import math
import ml_dtypes
import numpy as np
import jax
import jax.numpy as jnp
from jax import lax
from jax.experimental import pallas as pl
from jax.experimental.pallas import tpu as pltpu
from jax.sharding import PartitionSpec as P

HI = lax.Precision.HIGHEST


def slab_order(count):
    return np.concatenate([np.arange(0, count, 2), np.arange(1, count, 2)])


def slab_table(count):
    order = slab_order(count)
    cell = np.arange(count)
    table = math.sqrt(2.0 / count) * np.sin(np.pi * np.outer(order, cell) / count)
    table[0, 0] = 1.0
    return table


def sine_table(count):
    index = np.arange(1, count + 1)
    angle = np.outer(index, index) % (2 * (count + 1)) * (np.pi / (count + 1))
    return math.sqrt(2.0 / (count + 1)) * np.sin(angle)


def hartley_table(count):
    index = np.arange(count)
    angle = np.outer(index, index) % count * (2.0 * np.pi / count)
    return np.cos(angle) + np.sin(angle)


def wall_part(count):
    return np.sin(np.arange(1, count + 1) * (np.pi / (2 * count + 2))) ** 2


def shift_pair(block, axis, dim):
    count = lax.axis_size(axis)
    forward = [(i, (i + 1) % count) for i in range(count)]
    backward = [(target, source) for source, target in forward]
    low = lax.ppermute(lax.slice_in_dim(block, block.shape[dim] - 1, None, axis=dim), axis, forward)
    high = lax.ppermute(lax.slice_in_dim(block, 0, 1, axis=dim), axis, backward)
    return low, high


def owner(recv, ngx, ngz, n, m_cells, ny):
    nx, half = ngx * n, m_cells // 2
    mc = recv.shape[1]
    got = recv.reshape(ngx, ngz, mc, -1)
    a_end, b_end = got[..., :m_cells], got[..., m_cells:2 * m_cells]
    t_e, t_o, f_int = (got[..., 2 * m_cells + i * n:2 * m_cells + (i + 1) * n] for i in range(3))
    first = (lax.axis_index("gx") * ngz + lax.axis_index("gz")) * mc
    order = slab_order(m_cells)
    wall = lax.dynamic_slice_in_dim(jnp.asarray(wall_part(ny), jnp.float32), first, mc)
    across = jnp.asarray(np.sin(np.pi * order / (2 * m_cells)) ** 2, jnp.float32)
    s = jnp.sqrt(wall[:, None] + across)
    theta = 2.0 * jnp.log1p(s + s * s / (1.0 + jnp.sqrt(1.0 + s * s)))
    real = jnp.asarray(order > 0, jnp.float32)
    power = lambda e: jnp.exp(-theta * e)
    edge = jnp.asarray(slab_table(m_cells)[:, 1] * (order > 0), jnp.float32)
    steps = jnp.arange(n, dtype=jnp.float32)[None, :, None]
    rise = edge * jnp.exp(-theta[:, None, :] * (steps + 1.0))
    fall = edge * jnp.exp(-theta[:, None, :] * (n - 1.0 - steps))
    r_n = power(float(n)) * real
    wrap = 1.0 / (1.0 - power(float(nx)) * real)
    gain = real * power(1.0) / (1.0 - power(2.0))

    def carries(ends, back):
        seq = list(range(ngx))[::-1] if back else list(range(ngx))
        total = ends[seq[0]]
        for d in seq[1:]:
            total = r_n * total + ends[d]
        now = total * wrap
        out = [None] * ngx
        for d in seq:
            out[d] = now
            now = r_n * now + ends[d]
        return jnp.stack(out)

    def both(fn):
        return [fn(slice(0, half)), fn(slice(half, None))]

    a_in, b_in = carries(a_end, False), carries(b_end, True)
    add_e, add_o = both(lambda q: jnp.einsum("djmq,mxq->djmx", a_in[..., q] * gain[:, q], rise[..., q], precision=HI)
                        + jnp.einsum("djmq,mxq->djmx", b_in[..., q] * gain[:, q], fall[..., q], precision=HI))
    t_e, t_o = t_e - add_e, t_o - add_o
    rhs = f_int - (t_o + t_e) - jnp.roll(t_o - t_e, 1, 1)
    hx = jnp.asarray(hartley_table(nx), jnp.float32)
    hj = jnp.asarray(hartley_table(ngz), jnp.float32)
    line = jnp.einsum("djmx,ij->imdx", rhs, hj, precision=HI).reshape(ngz * mc, nx)
    spec = jnp.dot(line, hx, precision=HI).reshape(ngz, mc, nx)
    s2 = wall[:, None] + jnp.asarray(np.sin(np.pi * np.arange(nx) / nx) ** 2, jnp.float32)
    sq = jnp.sqrt(s2)
    root = jnp.sqrt(1.0 + s2)
    decay = jnp.exp(-2.0 * m_cells * jnp.log1p(sq + s2 / (1.0 + root)))
    cosj = jnp.asarray(np.cos(2 * np.pi * np.arange(ngz) / ngz), jnp.float32)[:, None, None]
    schur = -4.0 * sq * root * (1.0 + decay * decay - 2.0 * decay * cosj) / (1.0 - decay * decay)
    spec = spec / (schur * float(nx * ngz))
    line = jnp.dot(spec.reshape(ngz * mc, nx), hx, precision=HI).reshape(ngz, mc, nx)
    g = jnp.einsum("imx,ij->jmx", line, hj, precision=HI)
    g_next = jnp.roll(g, -1, 0)
    blocks = lambda f: jnp.moveaxis(f.reshape(ngz, mc, ngx, n), 2, 0)
    even, odd = blocks(g - g_next), blocks(g + g_next)
    pick = lambda t: jnp.concatenate([jnp.einsum("djmx,mxq->djmq", even, t[..., :half], precision=HI),
                                      jnp.einsum("djmx,mxq->djmq", odd, t[..., half:], precision=HI)], -1)
    a_in = carries(a_end - pick(fall), False)
    b_in = carries(b_end - pick(rise), True)

    def windows(f):
        wide = jnp.concatenate([f[..., -2:], f, f[..., :6]], -1)
        return jnp.stack([wide[..., d * n:d * n + n + 8] for d in range(ngx)])

    out = jnp.concatenate([a_in, b_in, windows(g), windows(g_next)], -1)
    return out.reshape(ngx * ngz, mc, -1)


VMEM_LIMIT = 60 * 1024 * 1024
EXTRA = 16


def split_np(table):
    wide = np.asarray(table, np.float32)
    high = wide.astype(ml_dtypes.bfloat16)
    low = (np.asarray(table, np.float64) - high.astype(np.float64)).astype(ml_dtypes.bfloat16)
    return jnp.asarray(high), jnp.asarray(low)


def split(value):
    high = value.astype(jnp.bfloat16)
    return high, (value - high.astype(jnp.float32)).astype(jnp.bfloat16)


def dot(a, b):
    return jnp.dot(a, b, preferred_element_type=jnp.float32)


def dot3(a, b):
    return dot(a[0], b[0]) + (dot(a[1], b[0]) + dot(a[0], b[1]))


def mode_planes(m_cells, ny):
    order = slab_order(m_cells)
    s = np.sqrt(np.sin(np.pi * order / (2 * m_cells))[:, None] ** 2 + wall_part(ny)[None])
    r = (np.sqrt(1 + s * s) - s) ** 2 * (order > 0)[:, None]
    edge = slab_table(m_cells)[:, 1] * (order > 0)
    edge = np.broadcast_to(edge[:, None], r.shape)
    return jnp.asarray(r, jnp.float32), jnp.asarray(edge, jnp.float32)


def chunks(rows, size=24):
    half = rows // 2
    size = math.gcd(size, half)
    return [slice(i, i + size) for i in range(0, rows, size)]


def wall_gap(field):
    ny = field.shape[1]
    at = lax.broadcasted_iota(jnp.int32, field.shape, 1)
    after = jnp.where(at == ny - 1, 0.0, pltpu.roll(field, ny - 1, 1))
    before = jnp.where(at == 0, 0.0, pltpu.roll(field, 1, 1))
    return after - before


def front_kernel(planes, steps, u_lo, u_hi, u_prev, u, u_next, v, w, w_lo, w_hi, sh, sl, th, tl, r, edge,
                 a_out, pay, a_all, now, xh, xl, hits):
    i = pl.program_id(0)
    mz, ny = now.shape
    n = planes * steps
    half = mz // 2
    f = lambda t: t.astype(jnp.float32)

    @pl.when(i == 0)
    def _():
        now[...] = jnp.zeros_like(now)

    row = lax.broadcasted_iota(jnp.int32, (mz, ny), 0)
    for p in range(planes):
        if p == 0:
            before = jnp.where(i == 0, f(u_lo[0]), f(u_prev[0]))
        else:
            before = f(u[p - 1])
        if p == planes - 1:
            after = jnp.where(i == steps - 1, f(u_hi[0]), f(u_next[0]))
        else:
            after = f(u[p + 1])
        mid = f(w[p])
        w_after = jnp.where(row == mz - 1, w_hi[p], pltpu.roll(mid, mz - 1, 0))
        w_before = jnp.where(row == 0, w_lo[p], pltpu.roll(mid, 1, 0))
        div = 0.5 * ((after - before) + (w_after - w_before) + wall_gap(f(v[p])))
        high, low = split(div)
        xh[p * mz:(p + 1) * mz, :] = high
        xl[p * mz:(p + 1) * mz, :] = low
    spec = dot3((xh[...], xl[...]), (sh[...], sl[...]))
    for p in range(planes):
        part = split(spec[p * mz:(p + 1) * mz])
        a = r[...] * now[...] + dot3((th[...], tl[...]), part)
        now[...] = a
        a_out[p] = a
        a_all[i * planes + p] = a

    @pl.when(i == steps - 1)
    def _():
        pay[0:mz, :] = now[...]
        hits[...] = jnp.zeros_like(hits)
        for rows in chunks(mz, 8):
            rr = r[rows, :]
            ee = edge[rows, :]
            side = 0 if rows.start < half else 1
            start = -(rr * rr / (1.0 - rr * rr)) * now[rows, :]

            def body(k, part):
                x = n - 1 - k
                part = rr * (part - a_all[x, rows, :])
                hits[side, x] = hits[side, x] + ee * part
                return part

            part = lax.fori_loop(0, n, body, start)
            pay[mz + rows.start:mz + rows.stop, :] = -(1.0 - rr * rr) * part
        pay[2 * mz:2 * mz + n, :] = jnp.sum(hits[0], axis=1)
        pay[2 * mz + n:2 * mz + 2 * n, :] = jnp.sum(hits[1], axis=1)
        for x in range(n):
            pay[2 * mz + 2 * n + x:2 * mz + 2 * n + x + 1, :] = a_all[x, 0:1, :]


def front(u, v, w, u_lo, u_hi, w_lo, w_hi):
    n, mz, ny = u.shape
    planes = 4
    steps = n // planes
    r, edge = mode_planes(mz, ny)
    whole = lambda a: pl.BlockSpec(a.shape, lambda i: (0,) * a.ndim, pipeline_mode=pl.Buffered(1))
    group = pl.BlockSpec((planes, mz, ny), lambda i: (i, 0, 0))
    lines = pl.BlockSpec((planes, 1, ny), lambda i: (i, 0, 0))
    tables = split_np(sine_table(ny)) + split_np(slab_table(mz)) + (r, edge)
    w_lo, w_hi = w_lo.astype(jnp.float32), w_hi.astype(jnp.float32)
    prev = pl.BlockSpec((1, mz, ny), lambda i: (jnp.maximum(i * planes - 1, 0), 0, 0))
    after = pl.BlockSpec((1, mz, ny), lambda i: (jnp.minimum(i * planes + planes, n - 1), 0, 0))
    rows = 2 * mz + 3 * n
    return pl.pallas_call(
        functools.partial(front_kernel, planes, steps),
        grid=(steps,),
        in_specs=[whole(u_lo), whole(u_hi), prev, group, after, group, group, lines, lines] + [whole(t) for t in tables],
        out_specs=[group, pl.BlockSpec((rows, ny), lambda i: (0, 0), pipeline_mode=pl.Buffered(1))],
        out_shape=[jax.ShapeDtypeStruct((n, mz, ny), jnp.float32), jax.ShapeDtypeStruct((rows, ny), jnp.float32)],
        scratch_shapes=[pltpu.VMEM((n, mz, ny), jnp.float32), pltpu.VMEM((mz, ny), jnp.float32),
                        pltpu.VMEM((planes * mz, ny), jnp.bfloat16), pltpu.VMEM((planes * mz, ny), jnp.bfloat16),
                        pltpu.VMEM((2, n, 8, ny), jnp.float32)],
        compiler_params=pltpu.CompilerParams(dimension_semantics=("arbitrary",), vmem_limit_bytes=VMEM_LIMIT),
        name="front",
    )(u_lo, u_hi, u, u, u, v, w, w_lo, w_hi, *tables)


def back_kernel(n, a_hbm, a_in, b_in, g, g_next, u, v, w, sh, sl, th, tl, r, edge, stiff,
                p_out, u_out, v_out, w_out, a_all, now, xh, xl, pbuf, sems):
    s = pl.program_id(0)
    mz, ny = now.shape
    half = mz // 2
    tall = mz + EXTRA

    @pl.when(s == 0)
    def _():
        copies = [pltpu.make_async_copy(a_hbm.at[x], a_all.at[x + 1], sems.at[x]) for x in range(n)]
        for copy in copies:
            copy.start()
        now[...] = a_in[...]
        a_all[0] = a_in[...]

        def body(x, carry):
            pltpu.make_async_copy(a_hbm.at[x], a_all.at[x + 1], sems.at[x]).wait()
            here, there = g[pl.ds(x + 2, 1), :], g_next[pl.ds(x + 2, 1), :]
            for rows in chunks(mz):
                mix = here - there if rows.start < half else here + there
                new = r[rows, :] * now[rows, :] - edge[rows, :] * mix
                now[rows, :] = new
                a_all[x + 1, rows, :] = a_all[x + 1, rows, :] + new
            return carry

        lax.fori_loop(0, n, body, 0)
        for rows in chunks(mz):
            rr = r[rows, :]
            now[rows, :] = -(rr * rr * a_all[n, rows, :] + b_in[rows, :]) / (1.0 - rr * rr)

    for t in range(2):
        x = n - 2 * s - t

        def advance():
            now[...] = r[...] * (now[...] - a_all[x + 1])

        if t == 0:
            pl.when(s > 0)(advance)
        else:
            advance()
        now[0:1, :] = g[pl.ds(x + 2, 1), :]
        pz = dot3((th[...], tl[...]), split(now[...]))
        now[0:1, :] = jnp.zeros((1, ny), jnp.float32)
        high, low = split(pz)
        base = t * tall
        xh[base:base + mz, :] = high
        xl[base:base + mz, :] = low
        under = (a_all[jnp.minimum(x + 1, n), 0:1, :] - pz[1:2, :] - g[pl.ds(x + 3, 1), :] - g[pl.ds(x + 1, 1), :]
                 + stiff[...] * g[pl.ds(x + 2, 1), :])
        at = lax.broadcasted_iota(jnp.int32, (EXTRA, ny), 0)
        extra = jnp.where(at == 0, g_next[pl.ds(x + 2, 1), :], jnp.where(at == EXTRA - 1, under, 0.0))
        high, low = split(extra)
        xh[base + mz:base + tall, :] = high
        xl[base + mz:base + tall, :] = low
    slot = lax.rem(s, 2)
    fresh = dot3((xh[...], xl[...]), (sh[...], sl[...]))
    for t in range(2):
        pbuf[slot, t] = fresh[t * tall:(t + 1) * tall]

    @pl.when(s > 0)
    def _():
        f = lambda a: a.astype(jnp.float32)
        trio = ((1, pbuf[1 - slot, 0, :mz], pbuf[1 - slot, 1], pbuf[slot, 0, :mz]),
                (0, pbuf[1 - slot, 1, :mz], pbuf[slot, 0], pbuf[slot, 1, :mz]))
        for k, after, full, before in trio:
            mid = full[:mz]
            p_out[k] = mid
            u_out[k] = f(u[k]) - 0.5 * (after - before)
            v_out[k] = f(v[k]) - 0.5 * wall_gap(mid)
            up, down = pltpu.roll(full, tall - 1, 0)[:mz], pltpu.roll(full, 1, 0)[:mz]
            w_out[k] = f(w[k]) - 0.5 * (up - down)


def back(a_loc, ret, u, v, w):
    n, mz, ny = u.shape
    ret = ret.T
    a_in, b_in = ret[:mz], ret[mz:2 * mz]
    g, g_next = ret[2 * mz:2 * mz + n + 8], ret[2 * mz + n + 8:]
    r, edge = mode_planes(mz, ny)
    stiff = jnp.asarray(4.0 + 4.0 * wall_part(ny)[None], jnp.float32)
    tables = split_np(sine_table(ny)) + split_np(slab_table(mz).T) + (r, edge, stiff)
    whole = lambda a: pl.BlockSpec(a.shape, lambda i: (0,) * a.ndim, pipeline_mode=pl.Buffered(1))
    pair = pl.BlockSpec((2, mz, ny), lambda s: (jnp.minimum(n // 2 - s, n // 2 - 1), 0, 0))
    shape = jax.ShapeDtypeStruct((n, mz, ny), jnp.float32)
    tall = mz + EXTRA
    return pl.pallas_call(
        functools.partial(back_kernel, n),
        grid=(n // 2 + 1,),
        in_specs=[pl.BlockSpec(memory_space=pl.ANY)] + [whole(t) for t in (a_in, b_in, g, g_next)] + [pair] * 3
        + [whole(t) for t in tables],
        out_specs=[pair] * 4,
        out_shape=[shape] * 4,
        scratch_shapes=[pltpu.VMEM((n + 1, mz, ny), jnp.float32), pltpu.VMEM((mz, ny), jnp.float32),
                        pltpu.VMEM((2 * tall, ny), jnp.bfloat16), pltpu.VMEM((2 * tall, ny), jnp.bfloat16),
                        pltpu.VMEM((2, 2, tall, ny), jnp.float32), pltpu.SemaphoreType.DMA((n,))],
        compiler_params=pltpu.CompilerParams(dimension_semantics=("arbitrary",), vmem_limit_bytes=VMEM_LIMIT),
        name="back",
    )(a_loc, a_in, b_in, g, g_next, u, v, w, *tables)


def on_device(u, v, w):
    n, mz, ny = u.shape
    ngx, ngz = lax.axis_size("gx"), lax.axis_size("gz")
    u_lo, u_hi = shift_pair(u, "gx", 0)
    w_lo, w_hi = shift_pair(w, "gz", 1)
    a_loc, pay = front(u, v, w, u_lo, u_hi, w_lo, w_hi)
    ndev = ngx * ngz
    got = lax.all_to_all(pay.T.reshape(ndev, ny // ndev, -1), ("gx", "gz"), 0, 0)
    send = owner(got, ngx, ngz, n, mz, ny)
    ret = lax.all_to_all(send, ("gx", "gz"), 0, 0).reshape(ny, -1)
    return back(a_loc, ret, u, v, w)


def solution(mesh):
    spec = P("gx", "gz", None)
    return jax.shard_map(on_device, mesh=mesh, in_specs=(spec,) * 3, out_specs=(spec,) * 4, check_vma=False)
```

```python
import functools
import math
import ml_dtypes
import numpy as np
import jax
import jax.numpy as jnp
from jax import lax
from jax.experimental import pallas as pl
from jax.experimental.pallas import tpu as pltpu
from jax.sharding import PartitionSpec as P

HI = lax.Precision.HIGHEST


def slab_order(count):
    return np.concatenate([np.arange(0, count, 2), np.arange(1, count, 2)])


def slab_table(count):
    order = slab_order(count)
    cell = np.arange(count)
    table = math.sqrt(2.0 / count) * np.sin(np.pi * np.outer(order, cell) / count)
    table[0, 0] = 1.0
    return table


def sine_table(count):
    index = np.arange(1, count + 1)
    angle = np.outer(index, index) % (2 * (count + 1)) * (np.pi / (count + 1))
    return math.sqrt(2.0 / (count + 1)) * np.sin(angle)


def hartley_table(count):
    index = np.arange(count)
    angle = np.outer(index, index) % count * (2.0 * np.pi / count)
    return np.cos(angle) + np.sin(angle)


def wall_part(count):
    return np.sin(np.arange(1, count + 1) * (np.pi / (2 * count + 2))) ** 2


def shift_pair(first, last, axis):
    count = lax.axis_size(axis)
    forward = [(i, (i + 1) % count) for i in range(count)]
    backward = [(target, source) for source, target in forward]
    return lax.ppermute(last, axis, forward), lax.ppermute(first, axis, backward)


VMEM_LIMIT = 60 * 1024 * 1024
EXTRA = 16


def split_np(table):
    wide = np.asarray(table, np.float32)
    high = wide.astype(ml_dtypes.bfloat16)
    low = (np.asarray(table, np.float64) - high.astype(np.float64)).astype(ml_dtypes.bfloat16)
    return jnp.asarray(high), jnp.asarray(low)


def split(value):
    high = value.astype(jnp.bfloat16)
    return high, (value - high.astype(jnp.float32)).astype(jnp.bfloat16)


def dot(a, b):
    return jnp.dot(a, b, preferred_element_type=jnp.float32)


def dot3(a, b):
    return dot(a[0], b[0]) + (dot(a[1], b[0]) + dot(a[0], b[1]))


def mode_planes(m_cells, ny):
    order = slab_order(m_cells)
    s = np.sqrt(np.sin(np.pi * order / (2 * m_cells))[:, None] ** 2 + wall_part(ny)[None])
    r = (np.sqrt(1 + s * s) - s) ** 2 * (order > 0)[:, None]
    edge = slab_table(m_cells)[:, 1] * (order > 0)
    edge = np.broadcast_to(edge[:, None], r.shape)
    return jnp.asarray(r, jnp.float32), jnp.asarray(edge, jnp.float32)


def round_up(count, unit=128):
    return -(-count // unit) * unit


def spans(mz, n):
    half, third = mz // 2, mz // 6
    return [(2 * mz, 2 * n), (0, third), (half, third), (mz, third), (mz + half, third)]


def width_of(mz, n):
    return 2 * mz + 2 * n + sum(size for _, size in spans(mz, n))


def pack(rows, mz, n):
    at = 2 * mz + 2 * n
    for start, size in spans(mz, n):
        value = rows[start:start + size, :]
        rows[at:at + size, :] = value - value.astype(jnp.bfloat16).astype(jnp.float32)
        at += size
    return rows[...].T.astype(jnp.bfloat16)


def unpack(rows, message, mz, n):
    rows[0:message.shape[1], :] = message[...].astype(jnp.float32).T
    at = 2 * mz + 2 * n
    for start, size in spans(mz, n):
        rows[start:start + size, :] = rows[start:start + size, :] + rows[at:at + size, :]
        at += size


def chunks(rows, size=24):
    half = rows // 2
    size = math.gcd(size, half)
    return [slice(i, i + size) for i in range(0, rows, size)]


def wall_gap(field):
    ny = field.shape[1]
    at = lax.broadcasted_iota(jnp.int32, field.shape, 1)
    after = jnp.where(at == ny - 1, 0.0, pltpu.roll(field, ny - 1, 1))
    before = jnp.where(at == 0, 0.0, pltpu.roll(field, 1, 1))
    return after - before


def front_kernel(planes, steps, u_lo, u_hi, u_prev, u, u_next, v, w, w_lo, w_hi, sh, sl, th, tl, r, edge,
                 a_out, pay_t, a_all, now, xa, xb, sa, sb, hits, pay, rims):
    i = pl.program_id(0)
    mz, ny = now.shape
    n = planes * steps
    half = mz // 2
    f = lambda t: t.astype(jnp.float32)

    def diverge(dst):
        row = lax.broadcasted_iota(jnp.int32, (mz, ny), 0)
        for p in range(planes):
            if p == 0:
                before = jnp.where(i == 0, f(u_lo[0]), f(u_prev[0]))
            else:
                before = f(u[p - 1])
            if p == planes - 1:
                after = jnp.where(i == steps - 1, f(u_hi[0]), f(u_next[0]))
            else:
                after = f(u[p + 1])
            mid = f(w[p])
            w_after = jnp.where(row == mz - 1, rims[1, pl.ds(i * planes + p, 1), :], pltpu.roll(mid, mz - 1, 0))
            w_before = jnp.where(row == 0, rims[0, pl.ds(i * planes + p, 1), :], pltpu.roll(mid, 1, 0))
            div = (after - before) + (w_after - w_before) + wall_gap(f(v[p]))
            high, low = split(div)
            dst[0, p * mz:(p + 1) * mz, :] = high
            dst[1, p * mz:(p + 1) * mz, :] = low

    def along_y(src, dst):
        lhs = jnp.concatenate([src[0], src[1], src[0]], axis=1)
        dst[...] = dot(lhs, jnp.concatenate([sh[...], sh[...], sl[...]], axis=0))

    def along_z(src):
        for p in range(planes):
            part = split(src[p * mz:(p + 1) * mz, :])
            right = jnp.concatenate([part[0], part[1], part[0]], axis=0)
            left = jnp.concatenate([th[...], th[...], tl[...]], axis=1)
            a = r[...] * now[...] + dot(left, right)
            now[...] = a
            a_out[p] = a
            a_all[(i - 2) * planes + p] = a

    xs, ss = (xa, xb), (sa, sb)

    @pl.when(i == 0)
    def _():
        now[...] = jnp.zeros_like(now)
        rims[0] = f(w_lo[...])
        rims[1] = f(w_hi[...])
        diverge(xa)

    @pl.when(i == 1)
    def _():
        along_y(xa, sa)
        diverge(xb)

    for par in range(2):
        @pl.when((i >= 2) & (i < steps) & (lax.rem(i, 2) == par))
        def _():
            along_y(xs[1 - par], ss[1 - par])
            diverge(xs[par])
            along_z(ss[par])

    @pl.when(i == steps)
    def _():
        along_y(xs[(steps - 1) % 2], ss[(steps - 1) % 2])
        along_z(ss[steps % 2])

    @pl.when(i == steps + 1)
    def _():
        along_z(ss[(steps + 1) % 2])
        pay[0:mz, :] = now[...]
        hits[...] = jnp.zeros_like(hits)
        for rows in chunks(mz, 16):
            rr = r[rows, :]
            ee = edge[rows, :]
            side = 0 if rows.start < half else 1
            start = -(rr * rr / (1.0 - rr * rr)) * now[rows, :]

            def body(k, part):
                x = n - 1 - k
                part = rr * (part - a_all[x, rows, :])
                add = ee * part
                total = add[0:8]
                for at in range(8, add.shape[0], 8):
                    total = total + add[at:at + 8]
                hits[side, x] = hits[side, x] + total
                return part

            part = lax.fori_loop(0, n, body, start, unroll=4)
            pay[mz + rows.start:mz + rows.stop, :] = -(1.0 - rr * rr) * part
        for x in range(n):
            pay[2 * mz + x:2 * mz + x + 1, :] = a_all[x, 0:1, :]
        t_e, t_o = jnp.sum(hits[0], axis=1), jnp.sum(hits[1], axis=1)
        pay[2 * mz:2 * mz + n, :] = pay[2 * mz:2 * mz + n, :] - (t_o + t_e)
        pay[2 * mz + n:2 * mz + 2 * n, :] = t_o - t_e
        pay_t[...] = pack(pay, mz, n)[:, 0:pay_t.shape[1]]


def front(u, v, w, u_lo, u_hi, w_lo, w_hi):
    n, mz, ny = u.shape
    planes = 2
    steps = n // planes
    r, edge = mode_planes(mz, ny)
    whole = lambda a: pl.BlockSpec(a.shape, lambda i: (0,) * a.ndim, pipeline_mode=pl.Buffered(1))
    here = lambda i: jnp.minimum(i, steps - 1)
    group = pl.BlockSpec((planes, mz, ny), lambda i: (here(i), 0, 0))
    tables = split_np(0.5 * sine_table(ny)) + split_np(slab_table(mz)) + (r, edge)
    prev = pl.BlockSpec((1, mz, ny), lambda i: (jnp.maximum(here(i) * planes - 1, 0), 0, 0))
    after = pl.BlockSpec((1, mz, ny), lambda i: (jnp.minimum(i * planes + planes, n - 1), 0, 0))
    rows = width_of(mz, n)
    return pl.pallas_call(
        functools.partial(front_kernel, planes, steps),
        grid=(steps + 2,),
        in_specs=[whole(u_lo), whole(u_hi), prev, group, after, group, group, whole(w_lo), whole(w_hi)] + [whole(t) for t in tables],
        out_specs=[pl.BlockSpec((planes, mz, ny), lambda i: (jnp.maximum(i - 2, 0), 0, 0)),
                   pl.BlockSpec((ny, rows), lambda i: (0, 0), pipeline_mode=pl.Buffered(1))],
        out_shape=[jax.ShapeDtypeStruct((n, mz, ny), jnp.float32), jax.ShapeDtypeStruct((ny, rows), jnp.bfloat16)],
        scratch_shapes=[pltpu.VMEM((n, mz, ny), jnp.float32), pltpu.VMEM((mz, ny), jnp.float32),
                        pltpu.VMEM((2, planes * mz, ny), jnp.bfloat16), pltpu.VMEM((2, planes * mz, ny), jnp.bfloat16),
                        pltpu.VMEM((planes * mz, ny), jnp.float32), pltpu.VMEM((planes * mz, ny), jnp.float32),
                        pltpu.VMEM((2, n, 8, ny), jnp.float32), pltpu.VMEM((round_up(rows), ny), jnp.float32),
                        pltpu.VMEM((2, n, ny), jnp.float32)],
        compiler_params=pltpu.CompilerParams(dimension_semantics=("arbitrary",), vmem_limit_bytes=VMEM_LIMIT),
        name="front",
    )(u_lo, u_hi, u, u, u, v, w, w_lo, w_hi, *tables)


def owner_kernel(ngx, ngz, n, recv, r, rn, wrap, gain, edge, first, last, inv, xh, xl, jh, jl,
                 out, buf, hits, mixed, res):
    mz, lanes = r.shape
    half = mz // 2
    mc = lanes // (ngx * ngz)
    step = ngz * mc
    unpack(buf, recv, mz, n)
    hits[...] = jnp.zeros_like(hits)

    def carries(up, down, rows):
        power = rn[rows, :]
        reach = 1
        while reach < ngx:
            up = up + power * pltpu.roll(up, step * reach, 1)
            down = down + power * pltpu.roll(down, lanes - step * reach, 1)
            reach *= 2
            if reach < ngx:
                power = power * power
        close = wrap[rows, :]
        return close * pltpu.roll(up, step, 1), close * pltpu.roll(down, lanes - step, 1)

    def fold(value):
        total = value[0:8]
        for at in range(8, value.shape[0], 8):
            total = total + value[at:at + 8]
        return total

    def below(rows):
        return slice(mz + rows.start, mz + rows.stop)

    for rows in chunks(mz, 16):
        up, down = carries(buf[rows, :], buf[below(rows), :], rows)
        res[rows, :] = gain[rows, :] * r[rows, :] * up
        res[below(rows), :] = gain[rows, :] * down
    for rows in chunks(mz, 32):
        rr = r[rows, :]
        side = 0 if rows.start < half else 1

        def rise(x, value):
            hits[0, side, x] = hits[0, side, x] + fold(value)
            return rr * value

        def fall(k, value):
            hits[1, side, n - 1 - k] = hits[1, side, n - 1 - k] + fold(value)
            return rr * value

        lax.fori_loop(0, n, rise, res[rows, :], unroll=4)
        lax.fori_loop(0, n, fall, res[below(rows), :], unroll=4)

    def beside(field, before):
        if ngz == 1:
            return field
        if before:
            return jnp.where(first[...] > 0.0, pltpu.roll(field, lanes - mc * (ngz - 1), 1), pltpu.roll(field, mc, 1))
        return jnp.where(last[...] > 0.0, pltpu.roll(field, mc * (ngz - 1), 1), pltpu.roll(field, lanes - mc, 1))

    t_e = jnp.sum(hits[0, 0] + hits[1, 0], axis=1)
    t_o = jnp.sum(hits[0, 1] + hits[1, 1], axis=1)
    own = buf[2 * mz:2 * mz + n, :] - (t_o + t_e)
    rhs = own - beside(buf[2 * mz + n:2 * mz + 2 * n, :] + (t_o - t_e), True)
    line = jnp.concatenate([rhs[:, d * step:(d + 1) * step] for d in range(ngx)], axis=0)
    across = (jh[...], jl[...])
    table = (xh[...], xl[...])
    line = dot3(split(line), across)
    line = dot3(table, split(line)) * inv[...]
    line = dot3(table, split(line))
    line = dot3(split(line), across)
    g = jnp.concatenate([line[d * n:(d + 1) * n] for d in range(ngx)], axis=1)
    g_next = beside(g, False)
    mixed[0] = g - g_next
    mixed[1] = g + g_next
    res[2 * mz:2 * mz + n, :] = g
    res[2 * mz + n:2 * mz + 2 * n, :] = g_next
    for rows in chunks(mz, 32):
        rr = r[rows, :]
        side = 0 if rows.start < half else 1
        zero = jnp.zeros_like(rr)
        up = lax.fori_loop(0, n, lambda x, t: rr * t + mixed[side, pl.ds(x, 1), :], zero, unroll=4)
        buf[rows, :] = buf[rows, :] - edge[rows, :] * up
        down = lax.fori_loop(0, n, lambda k, t: rr * (t + mixed[side, pl.ds(n - 1 - k, 1), :]), zero, unroll=4)
        buf[below(rows), :] = buf[below(rows), :] - edge[rows, :] * down
    for rows in chunks(mz, 16):
        up, down = carries(buf[rows, :], buf[below(rows), :], rows)
        res[rows, :] = up
        res[below(rows), :] = down
    res[0:1, :] = pltpu.roll(g[n - 1:n], step, 1)
    res[mz:mz + 1, :] = pltpu.roll(g[0:1], lanes - step, 1)
    out[...] = pack(res, mz, n)[:, 0:out.shape[1]]


def owner_tables(ngx, ngz, n, mz, ny):
    nx, ndev = ngx * n, ngx * ngz
    mc = ny // ndev
    start = (lax.axis_index("gx") * ngz + lax.axis_index("gz")) * mc
    order = slab_order(mz)
    wall = lax.dynamic_slice_in_dim(jnp.asarray(wall_part(ny), jnp.float32), start, mc)
    across = jnp.asarray(np.sin(np.pi * order / (2 * mz)) ** 2, jnp.float32)[:, None]
    real = jnp.asarray(order > 0, jnp.float32)[:, None]
    s = jnp.sqrt(wall + across)
    theta = 2.0 * jnp.log1p(s + s * s / (1.0 + jnp.sqrt(1.0 + s * s)))
    wide = lambda t: jnp.tile(t * real, (1, ndev))
    one = jnp.exp(-theta)
    edge = jnp.asarray(slab_table(mz)[:, 1:2], jnp.float32)
    r, rn = wide(one), wide(jnp.exp(-float(n) * theta))
    wrap = wide(1.0 / (1.0 - jnp.exp(-float(nx) * theta)))
    gain = wide(-edge * one / (1.0 - one * one))
    s2 = wall + jnp.asarray(np.sin(np.pi * np.arange(nx) / nx) ** 2, jnp.float32)[:, None]
    sq, root = jnp.sqrt(s2), jnp.sqrt(1.0 + s2)
    decay = jnp.exp(-2.0 * mz * jnp.log1p(sq + s2 / (1.0 + root)))
    inv = []
    for j in range(ngz):
        bend = 1.0 + decay * decay - 2.0 * math.cos(2.0 * math.pi * j / ngz) * decay
        inv.append(-(1.0 - decay * decay) / (4.0 * float(nx * ngz) * sq * root * bend))
    slab = np.arange(ny) // mc % ngz
    first = jnp.asarray((slab == 0)[None], jnp.float32)
    last = jnp.asarray((slab == ngz - 1)[None], jnp.float32)
    edge = mode_planes(mz, ny)[1]
    sides = split_np(hartley_table(nx)) + split_np(np.kron(hartley_table(ngz), np.eye(mc)))
    return (r, rn, wrap, gain, edge, first, last, jnp.concatenate(inv, axis=1)) + sides


def owner(recv, tables, ngx, ngz, n, mz):
    ny, width = recv.shape
    return pl.pallas_call(
        functools.partial(owner_kernel, ngx, ngz, n),
        out_shape=jax.ShapeDtypeStruct((ny, width), jnp.bfloat16),
        scratch_shapes=[pltpu.VMEM((round_up(width), ny), jnp.float32), pltpu.VMEM((2, 2, n, 8, ny), jnp.float32),
                        pltpu.VMEM((2, n, ny), jnp.float32), pltpu.VMEM((round_up(width), ny), jnp.float32)],
        compiler_params=pltpu.CompilerParams(vmem_limit_bytes=VMEM_LIMIT),
        name="owner",
    )(recv, *tables)


def back_kernel(n, a_hbm, ret, u, v, w, sh, sl, th, tl, r, edge, stiff,
                p_out, u_out, v_out, w_out, a_all, now, xa, xb, pa, pb, rt, rims, sems):
    s = pl.program_id(0)
    mz, ny = now.shape
    half = mz // 2
    tall = mz + EXTRA
    last = n // 2
    f = lambda a: a.astype(jnp.float32)
    line = lambda x: rims[pl.ds(x + 2, 1), :]
    line_next = lambda x: rt[pl.ds(2 * mz + n + jnp.clip(x, 0, n - 1), 1), :]

    def sweep():
        copies = [pltpu.make_async_copy(a_hbm.at[x], a_all.at[x + 1], sems.at[x]) for x in range(n)]
        for copy in copies:
            copy.start()
        unpack(rt, ret, mz, n)
        rims[...] = jnp.zeros_like(rims)
        rims[1:2, :] = rt[0:1, :]
        rims[2:2 + n, :] = rt[2 * mz:2 * mz + n, :]
        rims[2 + n:3 + n, :] = rt[mz:mz + 1, :]
        now[...] = rt[0:mz, :]
        a_all[0] = rt[0:mz, :]

        def body(x, carry):
            pltpu.make_async_copy(a_hbm.at[x], a_all.at[x + 1], sems.at[x]).wait()
            here, there = line(x), line_next(x)
            for rows in chunks(mz):
                mix = here - there if rows.start < half else here + there
                new = r[rows, :] * now[rows, :] - edge[rows, :] * mix
                now[rows, :] = new
                a_all[x + 1, rows, :] = a_all[x + 1, rows, :] + new
            return carry

        lax.fori_loop(0, n, body, 0)
        for rows in chunks(mz):
            rr = r[rows, :]
            b_in = rt[mz + rows.start:mz + rows.stop, :]
            now[rows, :] = -(rr * rr * a_all[n, rows, :] + b_in) / (1.0 - rr * rr)

    def along_z(dst, begin):
        for t in range(2):
            x = n - 2 * s - t
            if not (begin and t == 0):
                now[...] = r[...] * (now[...] - a_all[x + 1])
            now[0:1, :] = line(x)
            hat = split(now[...])
            now[0:1, :] = jnp.zeros((1, ny), jnp.float32)
            left = jnp.concatenate([th[...], th[...], tl[...]], axis=1)
            pz = dot(left, jnp.concatenate([hat[0], hat[1], hat[0]], axis=0))
            high, low = split(pz)
            base = t * tall
            dst[0, base:base + mz, :] = high
            dst[1, base:base + mz, :] = low
            under = (a_all[jnp.minimum(x + 1, n), 0:1, :] - pz[1:2, :] - line(x + 1) - line(x - 1)
                     + stiff[...] * line(x))
            at = lax.broadcasted_iota(jnp.int32, (EXTRA, ny), 0)
            extra = jnp.where(at == 0, line_next(x), jnp.where(at == EXTRA - 1, under, 0.0))
            high, low = split(extra)
            dst[0, base + mz:base + tall, :] = high
            dst[1, base + mz:base + tall, :] = low

    def along_y(src, dst):
        lhs = jnp.concatenate([src[0], src[1], src[0]], axis=1)
        fresh = dot(lhs, jnp.concatenate([sh[...], sh[...], sl[...]], axis=0))
        for t in range(2):
            dst[t] = fresh[t * tall:(t + 1) * tall]

    def finish(old, new):
        trio = ((1, old[0, :mz], old[1], new[0, :mz]), (0, old[1, :mz], new[0], new[1, :mz]))
        for k, after, full, before in trio:
            mid = full[:mz]
            p_out[k] = mid
            u_out[k] = f(u[k]) - 0.5 * (after - before)
            v_out[k] = f(v[k]) - 0.5 * wall_gap(mid)
            up, down = pltpu.roll(full, tall - 1, 0)[:mz], pltpu.roll(full, 1, 0)[:mz]
            w_out[k] = f(w[k]) - 0.5 * (up - down)

    xs, ps = (xa, xb), (pa, pb)

    @pl.when(s == 0)
    def _():
        sweep()
        along_z(xa, True)

    @pl.when(s == 1)
    def _():
        along_y(xa, pa)
        along_z(xb, False)

    for par in range(2):
        @pl.when((s >= 2) & (s <= last) & (lax.rem(s, 2) == par))
        def _():
            along_y(xs[1 - par], ps[1 - par])
            along_z(xs[par], False)
            finish(ps[par], ps[1 - par])

    @pl.when(s == last + 1)
    def _():
        along_y(xs[last % 2], ps[last % 2])
        finish(ps[1 - last % 2], ps[last % 2])


def back(a_loc, ret, u, v, w):
    n, mz, ny = u.shape
    r, edge = mode_planes(mz, ny)
    stiff = jnp.asarray(4.0 + 4.0 * wall_part(ny)[None], jnp.float32)
    tables = split_np(sine_table(ny)) + split_np(slab_table(mz).T) + (r, edge, stiff)
    whole = lambda a: pl.BlockSpec(a.shape, lambda i: (0,) * a.ndim, pipeline_mode=pl.Buffered(1))
    pair = pl.BlockSpec((2, mz, ny), lambda s: (jnp.clip(n // 2 + 1 - s, 0, n // 2 - 1), 0, 0))
    shape = jax.ShapeDtypeStruct((n, mz, ny), jnp.float32)
    tall = mz + EXTRA
    return pl.pallas_call(
        functools.partial(back_kernel, n),
        grid=(n // 2 + 2,),
        in_specs=[pl.BlockSpec(memory_space=pl.ANY), whole(ret)] + [pair] * 3 + [whole(t) for t in tables],
        out_specs=[pair] * 4,
        out_shape=[shape] * 4,
        scratch_shapes=[pltpu.VMEM((n + 1, mz, ny), jnp.float32), pltpu.VMEM((mz, ny), jnp.float32),
                        pltpu.VMEM((2, 2 * tall, ny), jnp.bfloat16), pltpu.VMEM((2, 2 * tall, ny), jnp.bfloat16),
                        pltpu.VMEM((2, tall, ny), jnp.float32), pltpu.VMEM((2, tall, ny), jnp.float32),
                        pltpu.VMEM((round_up(ret.shape[1]), ny), jnp.float32), pltpu.VMEM((n + 8, ny), jnp.float32),
                        pltpu.SemaphoreType.DMA((n,))],
        compiler_params=pltpu.CompilerParams(dimension_semantics=("arbitrary",), vmem_limit_bytes=VMEM_LIMIT),
        name="back",
    )(a_loc, ret, u, v, w, *tables)


def on_device(u, v, w):
    n, mz, ny = u.shape
    ngx, ngz = lax.axis_size("gx"), lax.axis_size("gz")
    ndev = ngx * ngz
    tables = owner_tables(ngx, ngz, n, mz, ny)
    w_lo, w_hi = shift_pair(w[:, 0], w[:, -1], "gz")
    u_lo, u_hi = shift_pair(u[:1], u[-1:], "gx")
    a_loc, pay = front(u, v, w, u_lo, u_hi, w_lo, w_hi)

    def swap(message):
        parts = message.reshape(ndev, ny // ndev, -1)
        return lax.all_to_all(parts, ("gx", "gz"), 0, 0).reshape(ny, -1)

    ret = swap(owner(swap(pay), tables, ngx, ngz, n, mz))
    return back(a_loc, ret, u, v, w)


def solution(mesh):
    spec = P("gx", "gz", None)
    return jax.shard_map(on_device, mesh=mesh, in_specs=(spec,) * 3, out_specs=(spec,) * 4, check_vma=False)
```

```python
import functools
import math
import ml_dtypes
import numpy as np
import jax
import jax.numpy as jnp
from jax import lax
from jax.experimental import pallas as pl
from jax.experimental.pallas import tpu as pltpu
from jax.sharding import PartitionSpec as P

HI = lax.Precision.HIGHEST


def slab_order(count):
    return np.concatenate([np.arange(0, count, 2), np.arange(1, count, 2)])


def slab_table(count):
    order = slab_order(count)
    cell = np.arange(count)
    table = math.sqrt(2.0 / count) * np.sin(np.pi * np.outer(order, cell) / count)
    table[0, 0] = 1.0
    return table


def sine_table(count):
    index = np.arange(1, count + 1)
    angle = np.outer(index, index) % (2 * (count + 1)) * (np.pi / (count + 1))
    return math.sqrt(2.0 / (count + 1)) * np.sin(angle)


def hartley_table(count):
    index = np.arange(count)
    angle = np.outer(index, index) % count * (2.0 * np.pi / count)
    return np.cos(angle) + np.sin(angle)


def wall_order(count, owners):
    places, each, third = np.arange(count // 2), count // owners, count // owners // 3
    owner, slot = places // each, places % each
    low = owner * third + slot
    high = count // 6 + owner * 2 * third + slot - third
    rank = np.where(slot < third, low, high)
    return np.concatenate([2 * rank, 2 * rank + 1])


def wall_part(count, owners):
    return np.sin((wall_order(count, owners) + 1) * (np.pi / (2 * count + 2))) ** 2


def folded_tables(count, owners, scale):
    table = scale * sine_table(count)[:count // 2, wall_order(count, owners)]
    return split_np(table[:, :count // 2]) + split_np(table[:, count // 2:])


def shift_pair(first, last, axis):
    count = lax.axis_size(axis)
    forward = [(i, (i + 1) % count) for i in range(count)]
    backward = [(target, source) for source, target in forward]
    return lax.ppermute(last, axis, forward), lax.ppermute(first, axis, backward)


VMEM_LIMIT = 60 * 1024 * 1024
EXTRA = 16


def split_np(table):
    wide = np.asarray(table, np.float32)
    high = wide.astype(ml_dtypes.bfloat16)
    low = (np.asarray(table, np.float64) - high.astype(np.float64)).astype(ml_dtypes.bfloat16)
    return jnp.asarray(high), jnp.asarray(low)


def split(value):
    high = value.astype(jnp.bfloat16)
    return high, (value - high.astype(jnp.float32)).astype(jnp.bfloat16)


def dot(a, b):
    return jnp.dot(a, b, preferred_element_type=jnp.float32)


def dot3(a, b):
    return dot(a[0], b[0]) + (dot(a[1], b[0]) + dot(a[0], b[1]))


def mode_planes(m_cells, ny, owners):
    order = slab_order(m_cells)
    s = np.sqrt(np.sin(np.pi * order / (2 * m_cells))[:, None] ** 2 + wall_part(ny, owners)[None])
    r = (np.sqrt(1 + s * s) - s) ** 2 * (order > 0)[:, None]
    edge = slab_table(m_cells)[:, 1] * (order > 0)
    edge = np.broadcast_to(edge[:, None], r.shape)
    return jnp.asarray(r, jnp.float32), jnp.asarray(edge, jnp.float32)


def round_up(count, unit=128):
    return -(-count // unit) * unit


def spans(mz, n):
    half, third = mz // 2, mz // 6
    return [(2 * mz, 2 * n), (0, third), (half, third), (mz, third), (mz + half, third)]


def piece_of(mz, n):
    return -(-sum(size for _, size in spans(mz, n)) // 24) * 8


def width_of(mz, n):
    return 2 * mz + 2 * n + piece_of(mz, n)


def slot_third(shape, mc):
    lane = lax.broadcasted_iota(jnp.int32, shape, 1)
    return lax.div(lax.rem(lane, mc), mc // 3)


def pack(rows, low, mz, n, mc):
    at, main, piece = 0, 2 * mz + 2 * n, piece_of(mz, n)
    lanes = rows.shape[1]
    low[...] = jnp.zeros_like(low)
    for start, size in spans(mz, n):
        value = rows[start:start + size, :]
        low[at:at + size, :] = value - value.astype(jnp.bfloat16).astype(jnp.float32)
        at += size
    third = slot_third((piece, lanes), mc)
    mix = jnp.where(third == 1, pltpu.roll(low[piece:2 * piece, :], mc // 3, 1), low[0:piece, :])
    mix = jnp.where(third == 2, pltpu.roll(low[2 * piece:3 * piece, :], mc // 3 * 2, 1), mix)
    rows[main:main + piece, :] = mix
    return rows[...].T.astype(jnp.bfloat16)


def unpack(rows, low, message, mz, n, mc):
    at, main, piece = 0, 2 * mz + 2 * n, piece_of(mz, n)
    lanes = rows.shape[1]
    rows[0:message.shape[1], :] = message[...].astype(jnp.float32).T
    first = slot_third((piece, lanes), mc) == 0
    mix = rows[main:main + piece, :]
    for k in range(3):
        moved = pltpu.roll(mix, lanes - k * (mc // 3), 1) if k else mix
        low[k * piece:(k + 1) * piece, :] = jnp.where(first, moved, 0.0)
    for start, size in spans(mz, n):
        rows[start:start + size, :] = rows[start:start + size, :] + low[at:at + size, :]
        at += size


def chunks(rows, size=24):
    half = rows // 2
    size = math.gcd(size, half)
    return [slice(i, i + size) for i in range(0, rows, size)]


def flip(field):
    rows, width = field.shape
    if width % 128:
        return jnp.flip(field, 1)
    at = 127 - lax.broadcasted_iota(jnp.int32, (rows, 128), 1)
    parts = [jnp.take_along_axis(field[:, k:k + 128], at, axis=1) for k in range(0, width, 128)]
    return jnp.concatenate(parts[::-1], axis=1)


def fold_dot(src, tables, out):
    middle = out.shape[1] // 2
    for k, (high, low) in enumerate((tables[:2], tables[2:])):
        cols = slice(k * middle, (k + 1) * middle)
        lhs = jnp.concatenate([src[0, :, cols], src[1, :, cols], src[0, :, cols]], axis=1)
        out[:, cols] = dot(lhs, jnp.concatenate([high[...], high[...], low[...]], axis=0))


def wall_gap(field):
    ny = field.shape[1]
    at = lax.broadcasted_iota(jnp.int32, field.shape, 1)
    after = jnp.where(at == ny - 1, 0.0, pltpu.roll(field, ny - 1, 1))
    before = jnp.where(at == 0, 0.0, pltpu.roll(field, 1, 1))
    return after - before


def front_kernel(planes, steps, mc, u_lo, u_hi, u_prev, u, u_next, v, w, w_lo, w_hi, eh, el, oh, ol, th, tl, r, edge,
                 a_out, pay_t, a_all, now, xa, xb, sa, sb, hits, pay, low, rims):
    i = pl.program_id(0)
    mz, ny = now.shape
    n = planes * steps
    half = mz // 2
    f = lambda t: t.astype(jnp.float32)

    def diverge(dst):
        row = lax.broadcasted_iota(jnp.int32, (mz, ny), 0)
        for p in range(planes):
            if p == 0:
                before = jnp.where(i == 0, f(u_lo[0]), f(u_prev[0]))
            else:
                before = f(u[p - 1])
            if p == planes - 1:
                after = jnp.where(i == steps - 1, f(u_hi[0]), f(u_next[0]))
            else:
                after = f(u[p + 1])
            mid = f(w[p])
            w_after = jnp.where(row == mz - 1, rims[1, pl.ds(i * planes + p, 1), :], pltpu.roll(mid, mz - 1, 0))
            w_before = jnp.where(row == 0, rims[0, pl.ds(i * planes + p, 1), :], pltpu.roll(mid, 1, 0))
            div = (after - before) + (w_after - w_before) + wall_gap(f(v[p]))
            left, right = div[:, :ny // 2], flip(div[:, ny // 2:])
            for cols, value in ((slice(0, ny // 2), left + right), (slice(ny // 2, ny), left - right)):
                high, rest = split(value)
                dst[0, p * mz:(p + 1) * mz, cols] = high
                dst[1, p * mz:(p + 1) * mz, cols] = rest

    def along_y(src, dst):
        fold_dot(src, (eh, el, oh, ol), dst)

    def along_z(src):
        for p in range(planes):
            part = split(src[p * mz:(p + 1) * mz, :])
            right = jnp.concatenate([part[0], part[1], part[0]], axis=0)
            left = jnp.concatenate([th[...], th[...], tl[...]], axis=1)
            a = r[...] * now[...] + dot(left, right)
            now[...] = a
            a_out[p] = a
            a_all[(i - 2) * planes + p] = a

    xs, ss = (xa, xb), (sa, sb)

    @pl.when(i == 0)
    def _():
        now[...] = jnp.zeros_like(now)
        rims[0] = f(w_lo[...])
        rims[1] = f(w_hi[...])
        diverge(xa)

    @pl.when(i == 1)
    def _():
        along_y(xa, sa)
        diverge(xb)

    for par in range(2):
        @pl.when((i >= 2) & (i < steps) & (lax.rem(i, 2) == par))
        def _():
            along_y(xs[1 - par], ss[1 - par])
            diverge(xs[par])
            along_z(ss[par])

    @pl.when(i == steps)
    def _():
        along_y(xs[(steps - 1) % 2], ss[(steps - 1) % 2])
        along_z(ss[steps % 2])

    @pl.when(i == steps + 1)
    def _():
        along_z(ss[(steps + 1) % 2])
        pay[0:mz, :] = now[...]
        hits[...] = jnp.zeros_like(hits)
        for rows in chunks(mz, 16):
            rr = r[rows, :]
            ee = edge[rows, :]
            side = 0 if rows.start < half else 1
            start = -(rr * rr / (1.0 - rr * rr)) * now[rows, :]

            def body(k, part):
                x = n - 1 - k
                part = rr * (part - a_all[x, rows, :])
                add = ee * part
                total = add[0:8]
                for at in range(8, add.shape[0], 8):
                    total = total + add[at:at + 8]
                hits[side, x] = hits[side, x] + total
                return part

            part = lax.fori_loop(0, n, body, start, unroll=4)
            pay[mz + rows.start:mz + rows.stop, :] = -(1.0 - rr * rr) * part
        for x in range(n):
            pay[2 * mz + x:2 * mz + x + 1, :] = a_all[x, 0:1, :]
        t_e, t_o = jnp.sum(hits[0], axis=1), jnp.sum(hits[1], axis=1)
        pay[2 * mz:2 * mz + n, :] = pay[2 * mz:2 * mz + n, :] - (t_o + t_e)
        pay[2 * mz + n:2 * mz + 2 * n, :] = t_o - t_e
        pay_t[...] = pack(pay, low, mz, n, mc)[:, 0:pay_t.shape[1]]


def front(u, v, w, u_lo, u_hi, w_lo, w_hi, owners):
    n, mz, ny = u.shape
    planes = 2
    steps = n // planes
    r, edge = mode_planes(mz, ny, owners)
    whole = lambda a: pl.BlockSpec(a.shape, lambda i: (0,) * a.ndim, pipeline_mode=pl.Buffered(1))
    here = lambda i: jnp.minimum(i, steps - 1)
    group = pl.BlockSpec((planes, mz, ny), lambda i: (here(i), 0, 0))
    tables = folded_tables(ny, owners, 0.5) + split_np(slab_table(mz)) + (r, edge)
    prev = pl.BlockSpec((1, mz, ny), lambda i: (jnp.maximum(here(i) * planes - 1, 0), 0, 0))
    after = pl.BlockSpec((1, mz, ny), lambda i: (jnp.minimum(i * planes + planes, n - 1), 0, 0))
    rows = width_of(mz, n)
    return pl.pallas_call(
        functools.partial(front_kernel, planes, steps, ny // owners),
        grid=(steps + 2,),
        in_specs=[whole(u_lo), whole(u_hi), prev, group, after, group, group, whole(w_lo), whole(w_hi)] + [whole(t) for t in tables],
        out_specs=[pl.BlockSpec((planes, mz, ny), lambda i: (jnp.maximum(i - 2, 0), 0, 0)),
                   pl.BlockSpec((ny, rows), lambda i: (0, 0), pipeline_mode=pl.Buffered(1))],
        out_shape=[jax.ShapeDtypeStruct((n, mz, ny), jnp.float32), jax.ShapeDtypeStruct((ny, rows), jnp.bfloat16)],
        scratch_shapes=[pltpu.VMEM((n, mz, ny), jnp.float32), pltpu.VMEM((mz, ny), jnp.float32),
                        pltpu.VMEM((2, planes * mz, ny), jnp.bfloat16), pltpu.VMEM((2, planes * mz, ny), jnp.bfloat16),
                        pltpu.VMEM((planes * mz, ny), jnp.float32), pltpu.VMEM((planes * mz, ny), jnp.float32),
                        pltpu.VMEM((2, n, 8, ny), jnp.float32), pltpu.VMEM((round_up(rows), ny), jnp.float32),
                        pltpu.VMEM((3 * piece_of(mz, n), ny), jnp.float32), pltpu.VMEM((2, n, ny), jnp.float32)],
        compiler_params=pltpu.CompilerParams(dimension_semantics=("arbitrary",), vmem_limit_bytes=VMEM_LIMIT),
        name="front",
    )(u_lo, u_hi, u, u, u, v, w, w_lo, w_hi, *tables)


def owner_kernel(ngx, ngz, n, recv, r, rn, wrap, gain, edge, first, last, inv, xh, xl, jh, jl,
                 out, buf, hits, mixed, res, low):
    mz, lanes = r.shape
    half = mz // 2
    mc = lanes // (ngx * ngz)
    step = ngz * mc
    unpack(buf, low, recv, mz, n, mc)
    hits[...] = jnp.zeros_like(hits)

    def carries(up, down, rows):
        power = rn[rows, :]
        reach = 1
        while reach < ngx:
            up = up + power * pltpu.roll(up, step * reach, 1)
            down = down + power * pltpu.roll(down, lanes - step * reach, 1)
            reach *= 2
            if reach < ngx:
                power = power * power
        close = wrap[rows, :]
        return close * pltpu.roll(up, step, 1), close * pltpu.roll(down, lanes - step, 1)

    def fold(value):
        total = value[0:8]
        for at in range(8, value.shape[0], 8):
            total = total + value[at:at + 8]
        return total

    def below(rows):
        return slice(mz + rows.start, mz + rows.stop)

    for rows in chunks(mz, 16):
        up, down = carries(buf[rows, :], buf[below(rows), :], rows)
        res[rows, :] = gain[rows, :] * r[rows, :] * up
        res[below(rows), :] = gain[rows, :] * down
    for rows in chunks(mz, 32):
        rr = r[rows, :]
        side = 0 if rows.start < half else 1

        def rise(x, value):
            hits[0, side, x] = hits[0, side, x] + fold(value)
            return rr * value

        def fall(k, value):
            hits[1, side, n - 1 - k] = hits[1, side, n - 1 - k] + fold(value)
            return rr * value

        lax.fori_loop(0, n, rise, res[rows, :], unroll=True)
        lax.fori_loop(0, n, fall, res[below(rows), :], unroll=True)

    def beside(field, before):
        if ngz == 1:
            return field
        if before:
            return jnp.where(first[...] > 0.0, pltpu.roll(field, lanes - mc * (ngz - 1), 1), pltpu.roll(field, mc, 1))
        return jnp.where(last[...] > 0.0, pltpu.roll(field, mc * (ngz - 1), 1), pltpu.roll(field, lanes - mc, 1))

    t_e = jnp.sum(hits[0, 0] + hits[1, 0], axis=1)
    t_o = jnp.sum(hits[0, 1] + hits[1, 1], axis=1)
    own = buf[2 * mz:2 * mz + n, :] - (t_o + t_e)
    rhs = own - beside(buf[2 * mz + n:2 * mz + 2 * n, :] + (t_o - t_e), True)
    line = jnp.concatenate([rhs[:, d * step:(d + 1) * step] for d in range(ngx)], axis=0)
    across = (jh[...], jl[...])
    table = (xh[...], xl[...])
    line = dot3(split(line), across)
    line = dot3(table, split(line)) * inv[...]
    line = dot3(table, split(line))
    line = dot3(split(line), across)
    g = jnp.concatenate([line[d * n:(d + 1) * n] for d in range(ngx)], axis=1)
    g_next = beside(g, False)
    mixed[0] = g - g_next
    mixed[1] = g + g_next
    res[2 * mz:2 * mz + n, :] = g
    res[2 * mz + n:2 * mz + 2 * n, :] = g_next
    for rows in chunks(mz, 32):
        rr = r[rows, :]
        side = 0 if rows.start < half else 1
        zero = jnp.zeros_like(rr)
        up = lax.fori_loop(0, n, lambda x, t: rr * t + mixed[side, pl.ds(x, 1), :], zero, unroll=True)
        buf[rows, :] = buf[rows, :] - edge[rows, :] * up
        down = lax.fori_loop(0, n, lambda k, t: rr * (t + mixed[side, pl.ds(n - 1 - k, 1), :]), zero, unroll=True)
        buf[below(rows), :] = buf[below(rows), :] - edge[rows, :] * down
    for rows in chunks(mz, 16):
        up, down = carries(buf[rows, :], buf[below(rows), :], rows)
        res[rows, :] = up
        res[below(rows), :] = down
    res[0:1, :] = pltpu.roll(g[n - 1:n], step, 1)
    res[mz:mz + 1, :] = pltpu.roll(g[0:1], lanes - step, 1)
    out[...] = pack(res, low, mz, n, mc)[:, 0:out.shape[1]]


def owner_tables(ngx, ngz, n, mz, ny):
    nx, ndev = ngx * n, ngx * ngz
    mc = ny // ndev
    start = (lax.axis_index("gx") * ngz + lax.axis_index("gz")) * mc
    order = slab_order(mz)
    wall = lax.dynamic_slice_in_dim(jnp.asarray(wall_part(ny, ndev), jnp.float32), start, mc)
    across = jnp.asarray(np.sin(np.pi * order / (2 * mz)) ** 2, jnp.float32)[:, None]
    real = jnp.asarray(order > 0, jnp.float32)[:, None]
    s = jnp.sqrt(wall + across)
    theta = 2.0 * jnp.log1p(s + s * s / (1.0 + jnp.sqrt(1.0 + s * s)))
    wide = lambda t: jnp.tile(t * real, (1, ndev))
    one = jnp.exp(-theta)
    edge = jnp.asarray(slab_table(mz)[:, 1:2], jnp.float32)
    r, rn = wide(one), wide(jnp.exp(-float(n) * theta))
    wrap = wide(1.0 / (1.0 - jnp.exp(-float(nx) * theta)))
    gain = wide(-edge * one / (1.0 - one * one))
    s2 = wall + jnp.asarray(np.sin(np.pi * np.arange(nx) / nx) ** 2, jnp.float32)[:, None]
    sq, root = jnp.sqrt(s2), jnp.sqrt(1.0 + s2)
    decay = jnp.exp(-2.0 * mz * jnp.log1p(sq + s2 / (1.0 + root)))
    inv = []
    for j in range(ngz):
        bend = 1.0 + decay * decay - 2.0 * math.cos(2.0 * math.pi * j / ngz) * decay
        inv.append(-(1.0 - decay * decay) / (4.0 * float(nx * ngz) * sq * root * bend))
    slab = np.arange(ny) // mc % ngz
    first = jnp.asarray((slab == 0)[None], jnp.float32)
    last = jnp.asarray((slab == ngz - 1)[None], jnp.float32)
    edge = mode_planes(mz, ny, ndev)[1]
    sides = split_np(hartley_table(nx)) + split_np(np.kron(hartley_table(ngz), np.eye(mc)))
    return (r, rn, wrap, gain, edge, first, last, jnp.concatenate(inv, axis=1)) + sides


def owner(recv, tables, ngx, ngz, n, mz):
    ny, width = recv.shape
    return pl.pallas_call(
        functools.partial(owner_kernel, ngx, ngz, n),
        out_shape=jax.ShapeDtypeStruct((ny, width), jnp.bfloat16),
        scratch_shapes=[pltpu.VMEM((round_up(width), ny), jnp.float32), pltpu.VMEM((2, 2, n, 8, ny), jnp.float32),
                        pltpu.VMEM((2, n, ny), jnp.float32), pltpu.VMEM((round_up(width), ny), jnp.float32),
                        pltpu.VMEM((3 * piece_of(mz, n), ny), jnp.float32)],
        compiler_params=pltpu.CompilerParams(vmem_limit_bytes=VMEM_LIMIT),
        name="owner",
    )(recv, *tables)


def back_kernel(n, mc, a_hbm, ret, u, v, w, eh, el, oh, ol, th, tl, r, edge, stiff,
                p_out, u_out, v_out, w_out, a_all, now, xa, xb, pa, pb, rt, low, rims, modes, sems):
    s = pl.program_id(0)
    mz, ny = now.shape
    half = mz // 2
    tall = mz + EXTRA
    last = n // 2
    f = lambda a: a.astype(jnp.float32)
    line = lambda x: rims[pl.ds(x + 2, 1), :]
    line_next = lambda x: rt[pl.ds(2 * mz + n + jnp.clip(x, 0, n - 1), 1), :]

    def sweep():
        copies = [pltpu.make_async_copy(a_hbm.at[x], a_all.at[x + 1], sems.at[x]) for x in range(n)]
        for copy in copies:
            copy.start()
        unpack(rt, low, ret, mz, n, mc)
        rims[...] = jnp.zeros_like(rims)
        rims[1:2, :] = rt[0:1, :]
        rims[2:2 + n, :] = rt[2 * mz:2 * mz + n, :]
        rims[2 + n:3 + n, :] = rt[mz:mz + 1, :]
        now[...] = rt[0:mz, :]
        a_all[0] = rt[0:mz, :]

        def body(x, carry):
            pltpu.make_async_copy(a_hbm.at[x], a_all.at[x + 1], sems.at[x]).wait()
            here, there = line(x), line_next(x)
            for rows in chunks(mz):
                mix = here - there if rows.start < half else here + there
                new = r[rows, :] * now[rows, :] - edge[rows, :] * mix
                now[rows, :] = new
                a_all[x + 1, rows, :] = a_all[x + 1, rows, :] + new
            return carry

        lax.fori_loop(0, n, body, 0)
        for rows in chunks(mz):
            rr = r[rows, :]
            b_in = rt[mz + rows.start:mz + rows.stop, :]
            now[rows, :] = -(rr * rr * a_all[n, rows, :] + b_in) / (1.0 - rr * rr)

    def along_z(dst, begin):
        for t in range(2):
            x = n - 2 * s - t
            if not (begin and t == 0):
                now[...] = r[...] * (now[...] - a_all[x + 1])
            now[0:1, :] = line(x)
            hat = split(now[...])
            now[0:1, :] = jnp.zeros((1, ny), jnp.float32)
            left = jnp.concatenate([th[...], th[...], tl[...]], axis=1)
            pz = dot(left, jnp.concatenate([hat[0], hat[1], hat[0]], axis=0))
            high, rest = split(pz)
            base = t * tall
            dst[0, base:base + mz, :] = high
            dst[1, base:base + mz, :] = rest
            under = (a_all[jnp.minimum(x + 1, n), 0:1, :] - pz[1:2, :] - line(x + 1) - line(x - 1)
                     + stiff[...] * line(x))
            at = lax.broadcasted_iota(jnp.int32, (EXTRA, ny), 0)
            extra = jnp.where(at == 0, line_next(x), jnp.where(at == EXTRA - 1, under, 0.0))
            high, rest = split(extra)
            dst[0, base + mz:base + tall, :] = high
            dst[1, base + mz:base + tall, :] = rest

    def along_y(src, dst):
        fold_dot(src, (eh, el, oh, ol), modes)
        for t in range(2):
            rows = slice(t * tall, (t + 1) * tall)
            even, odd = modes[rows, :ny // 2], modes[rows, ny // 2:]
            dst[t, :, :ny // 2] = even + odd
            dst[t, :, ny // 2:] = flip(even - odd)

    def finish(old, new):
        trio = ((1, old[0, :mz], old[1], new[0, :mz]), (0, old[1, :mz], new[0], new[1, :mz]))
        for k, after, full, before in trio:
            mid = full[:mz]
            p_out[k] = mid
            u_out[k] = f(u[k]) - 0.5 * (after - before)
            v_out[k] = f(v[k]) - 0.5 * wall_gap(mid)
            up, down = pltpu.roll(full, tall - 1, 0)[:mz], pltpu.roll(full, 1, 0)[:mz]
            w_out[k] = f(w[k]) - 0.5 * (up - down)

    xs, ps = (xa, xb), (pa, pb)

    @pl.when(s == 0)
    def _():
        sweep()
        along_z(xa, True)

    @pl.when(s == 1)
    def _():
        along_y(xa, pa)
        along_z(xb, False)

    for par in range(2):
        @pl.when((s >= 2) & (s <= last) & (lax.rem(s, 2) == par))
        def _():
            along_y(xs[1 - par], ps[1 - par])
            along_z(xs[par], False)
            finish(ps[par], ps[1 - par])

    @pl.when(s == last + 1)
    def _():
        along_y(xs[last % 2], ps[last % 2])
        finish(ps[1 - last % 2], ps[last % 2])


def back(a_loc, ret, u, v, w, owners):
    n, mz, ny = u.shape
    r, edge = mode_planes(mz, ny, owners)
    stiff = jnp.asarray(4.0 + 4.0 * wall_part(ny, owners)[None], jnp.float32)
    tables = tuple(t.T for t in folded_tables(ny, owners, 1.0)) + split_np(slab_table(mz).T) + (r, edge, stiff)
    whole = lambda a: pl.BlockSpec(a.shape, lambda i: (0,) * a.ndim, pipeline_mode=pl.Buffered(1))
    pair = pl.BlockSpec((2, mz, ny), lambda s: (jnp.clip(n // 2 + 1 - s, 0, n // 2 - 1), 0, 0))
    shape = jax.ShapeDtypeStruct((n, mz, ny), jnp.float32)
    tall = mz + EXTRA
    return pl.pallas_call(
        functools.partial(back_kernel, n, ny // owners),
        grid=(n // 2 + 2,),
        in_specs=[pl.BlockSpec(memory_space=pl.ANY), whole(ret)] + [pair] * 3 + [whole(t) for t in tables],
        out_specs=[pair] * 4,
        out_shape=[shape] * 4,
        scratch_shapes=[pltpu.VMEM((n + 1, mz, ny), jnp.float32), pltpu.VMEM((mz, ny), jnp.float32),
                        pltpu.VMEM((2, 2 * tall, ny), jnp.bfloat16), pltpu.VMEM((2, 2 * tall, ny), jnp.bfloat16),
                        pltpu.VMEM((2, tall, ny), jnp.float32), pltpu.VMEM((2, tall, ny), jnp.float32),
                        pltpu.VMEM((round_up(ret.shape[1]), ny), jnp.float32),
                        pltpu.VMEM((3 * piece_of(mz, n), ny), jnp.float32), pltpu.VMEM((n + 8, ny), jnp.float32),
                        pltpu.VMEM((2 * tall, ny), jnp.float32), pltpu.SemaphoreType.DMA((n,))],
        compiler_params=pltpu.CompilerParams(dimension_semantics=("arbitrary",), vmem_limit_bytes=VMEM_LIMIT),
        name="back",
    )(a_loc, ret, u, v, w, *tables)


def on_device(u, v, w):
    n, mz, ny = u.shape
    ngx, ngz = lax.axis_size("gx"), lax.axis_size("gz")
    ndev = ngx * ngz
    tables = owner_tables(ngx, ngz, n, mz, ny)
    w_lo, w_hi = shift_pair(w[:, 0], w[:, -1], "gz")
    u_lo, u_hi = shift_pair(u[:1], u[-1:], "gx")
    a_loc, pay = front(u, v, w, u_lo, u_hi, w_lo, w_hi, ndev)

    def swap(message):
        parts = message.reshape(ndev, ny // ndev, -1)
        return lax.all_to_all(parts, ("gx", "gz"), 0, 0).reshape(ny, -1)

    ret = swap(owner(swap(pay), tables, ngx, ngz, n, mz))
    return back(a_loc, ret, u, v, w, ndev)


def solution(mesh):
    spec = P("gx", "gz", None)
    return jax.shard_map(on_device, mesh=mesh, in_specs=(spec,) * 3, out_specs=(spec,) * 4, check_vma=False)
```

```python
import functools
import math
import ml_dtypes
import numpy as np
import jax
import jax.numpy as jnp
from jax import lax
from jax.experimental import pallas as pl
from jax.experimental.pallas import tpu as pltpu
from jax.sharding import PartitionSpec as P

HI = lax.Precision.HIGHEST


def slab_order(count):
    return np.concatenate([np.arange(0, count, 2), np.arange(1, count, 2)])


def slab_table(count):
    order = slab_order(count)
    cell = np.arange(count)
    table = math.sqrt(2.0 / count) * np.sin(np.pi * np.outer(order, cell) / count)
    table[0, 0] = 1.0
    return table


def sine_table(count):
    index = np.arange(1, count + 1)
    angle = np.outer(index, index) % (2 * (count + 1)) * (np.pi / (count + 1))
    return math.sqrt(2.0 / (count + 1)) * np.sin(angle)


def hartley_table(count):
    index = np.arange(count)
    angle = np.outer(index, index) % count * (2.0 * np.pi / count)
    return np.cos(angle) + np.sin(angle)


def wall_order(count, owners):
    places, each, third = np.arange(count // 2), count // owners, count // owners // 3
    owner, slot = places // each, places % each
    low = owner * third + slot
    high = count // 6 + owner * 2 * third + slot - third
    rank = np.where(slot < third, low, high)
    return np.concatenate([2 * rank, 2 * rank + 1])


def wall_part(count, owners):
    return np.sin((wall_order(count, owners) + 1) * (np.pi / (2 * count + 2))) ** 2


def folded_tables(count, owners, scale):
    table = scale * sine_table(count)[:count // 2, wall_order(count, owners)]
    return split_np(table[:, :count // 2]) + split_np(table[:, count // 2:])


def shift_pair(first, last, axis):
    count = lax.axis_size(axis)
    forward = [(i, (i + 1) % count) for i in range(count)]
    backward = [(target, source) for source, target in forward]
    return lax.ppermute(last, axis, forward), lax.ppermute(first, axis, backward)


VMEM_LIMIT = 60 * 1024 * 1024
EXTRA = 16


def split_np(table):
    wide = np.asarray(table, np.float32)
    high = wide.astype(ml_dtypes.bfloat16)
    low = (np.asarray(table, np.float64) - high.astype(np.float64)).astype(ml_dtypes.bfloat16)
    return jnp.asarray(high), jnp.asarray(low)


def split(value):
    high = value.astype(jnp.bfloat16)
    return high, (value - high.astype(jnp.float32)).astype(jnp.bfloat16)


def dot(a, b):
    return jnp.dot(a, b, preferred_element_type=jnp.float32)


def dot3(a, b):
    return dot(a[0], b[0]) + (dot(a[1], b[0]) + dot(a[0], b[1]))


def mode_planes(m_cells, ny, owners):
    order = slab_order(m_cells)
    s = np.sqrt(np.sin(np.pi * order / (2 * m_cells))[:, None] ** 2 + wall_part(ny, owners)[None])
    r = (np.sqrt(1 + s * s) - s) ** 2 * (order > 0)[:, None]
    edge = slab_table(m_cells)[:, 1] * (order > 0)
    edge = np.broadcast_to(edge[:, None], r.shape)
    return jnp.asarray(r, jnp.float32), jnp.asarray(edge, jnp.float32)


def round_up(count, unit=128):
    return -(-count // unit) * unit


def spans(mz, n):
    half, third = mz // 2, mz // 6
    return [(2 * mz, 2 * n), (0, third), (half, third), (mz, third), (mz + half, third)]


def piece_of(mz, n):
    return -(-sum(size for _, size in spans(mz, n)) // 24) * 8


def width_of(mz, n):
    return 2 * mz + 2 * n + piece_of(mz, n)


def slot_third(shape, mc):
    lane = lax.broadcasted_iota(jnp.int32, shape, 1)
    return lax.div(lax.rem(lane, mc), mc // 3)


def pack(rows, low, mz, n, mc):
    at, main, piece = 0, 2 * mz + 2 * n, piece_of(mz, n)
    lanes = rows.shape[1]
    low[...] = jnp.zeros_like(low)
    for start, size in spans(mz, n):
        value = rows[start:start + size, :]
        low[at:at + size, :] = value - value.astype(jnp.bfloat16).astype(jnp.float32)
        at += size
    third = slot_third((piece, lanes), mc)
    mix = jnp.where(third == 1, pltpu.roll(low[piece:2 * piece, :], mc // 3, 1), low[0:piece, :])
    mix = jnp.where(third == 2, pltpu.roll(low[2 * piece:3 * piece, :], mc // 3 * 2, 1), mix)
    rows[main:main + piece, :] = mix
    return rows[...].T.astype(jnp.bfloat16)


def unpack(rows, low, message, mz, n, mc):
    at, main, piece = 0, 2 * mz + 2 * n, piece_of(mz, n)
    lanes = rows.shape[1]
    rows[0:message.shape[1], :] = message[...].astype(jnp.float32).T
    first = slot_third((piece, lanes), mc) == 0
    mix = rows[main:main + piece, :]
    for k in range(3):
        moved = pltpu.roll(mix, lanes - k * (mc // 3), 1) if k else mix
        low[k * piece:(k + 1) * piece, :] = jnp.where(first, moved, 0.0)
    for start, size in spans(mz, n):
        rows[start:start + size, :] = rows[start:start + size, :] + low[at:at + size, :]
        at += size


def chunks(rows, size=24):
    half = rows // 2
    size = math.gcd(size, half)
    return [slice(i, i + size) for i in range(0, rows, size)]


def flip(field):
    rows, width = field.shape
    if width % 128:
        return jnp.flip(field, 1)
    at = 127 - lax.broadcasted_iota(jnp.int32, (rows, 128), 1)
    parts = [jnp.take_along_axis(field[:, k:k + 128], at, axis=1) for k in range(0, width, 128)]
    return jnp.concatenate(parts[::-1], axis=1)


def fold_dot(src, tables, out):
    middle = out.shape[1] // 2
    for k, (high, low) in enumerate((tables[:2], tables[2:])):
        cols = slice(k * middle, (k + 1) * middle)
        lhs = jnp.concatenate([src[0, :, cols], src[1, :, cols], src[0, :, cols]], axis=1)
        out[:, cols] = dot(lhs, jnp.concatenate([high[...], high[...], low[...]], axis=0))


def wall_gap(field):
    ny = field.shape[1]
    at = lax.broadcasted_iota(jnp.int32, field.shape, 1)
    after = jnp.where(at == ny - 1, 0.0, pltpu.roll(field, ny - 1, 1))
    before = jnp.where(at == 0, 0.0, pltpu.roll(field, 1, 1))
    return after - before


def front_kernel(planes, steps, mc, u_lo, u_hi, u_prev, u, u_next, v, w, w_lo, w_hi, eh, el, oh, ol, th, tl, r, edge,
                 a_out, pay_t, a_all, now, xa, xb, sa, sb, hits, pay, low, rims):
    i = pl.program_id(0)
    mz, ny = now.shape
    n = planes * steps
    half = mz // 2
    f = lambda t: t.astype(jnp.float32)

    def diverge(dst):
        row = lax.broadcasted_iota(jnp.int32, (mz, ny), 0)
        for p in range(planes):
            if p == 0:
                before = jnp.where(i == 0, f(u_lo[0]), f(u_prev[0]))
            else:
                before = f(u[p - 1])
            if p == planes - 1:
                after = jnp.where(i == steps - 1, f(u_hi[0]), f(u_next[0]))
            else:
                after = f(u[p + 1])
            mid = f(w[p])
            w_after = jnp.where(row == mz - 1, rims[1, pl.ds(i * planes + p, 1), :], pltpu.roll(mid, mz - 1, 0))
            w_before = jnp.where(row == 0, rims[0, pl.ds(i * planes + p, 1), :], pltpu.roll(mid, 1, 0))
            div = (after - before) + (w_after - w_before) + wall_gap(f(v[p]))
            left, right = div[:, :ny // 2], flip(div[:, ny // 2:])
            for cols, value in ((slice(0, ny // 2), left + right), (slice(ny // 2, ny), left - right)):
                high, rest = split(value)
                dst[0, p * mz:(p + 1) * mz, cols] = high
                dst[1, p * mz:(p + 1) * mz, cols] = rest

    def along_y(src, dst):
        fold_dot(src, (eh, el, oh, ol), dst)

    def along_z(src):
        for p in range(planes):
            part = split(src[p * mz:(p + 1) * mz, :])
            right = jnp.concatenate([part[0], part[1], part[0]], axis=0)
            left = jnp.concatenate([th[...], th[...], tl[...]], axis=1)
            a = r[...] * now[...] + dot(left, right)
            now[...] = a
            a_out[p] = a
            a_all[(i - 2) * planes + p] = a

    xs, ss = (xa, xb), (sa, sb)

    @pl.when(i == 0)
    def _():
        now[...] = jnp.zeros_like(now)
        rims[0] = f(w_lo[...])
        rims[1] = f(w_hi[...])
        diverge(xa)

    @pl.when(i == 1)
    def _():
        along_y(xa, sa)
        diverge(xb)

    for par in range(2):
        @pl.when((i >= 2) & (i < steps) & (lax.rem(i, 2) == par))
        def _():
            along_y(xs[1 - par], ss[1 - par])
            diverge(xs[par])
            along_z(ss[par])

    @pl.when(i == steps)
    def _():
        along_y(xs[(steps - 1) % 2], ss[(steps - 1) % 2])
        along_z(ss[steps % 2])

    @pl.when(i == steps + 1)
    def _():
        along_z(ss[(steps + 1) % 2])
        pay[0:mz, :] = now[...]
        hits[...] = jnp.zeros_like(hits)
        for rows in chunks(mz, 16):
            rr = r[rows, :]
            ee = edge[rows, :]
            side = 0 if rows.start < half else 1
            start = -(rr * rr / (1.0 - rr * rr)) * now[rows, :]

            def body(k, part):
                x = n - 1 - k
                part = rr * (part - a_all[x, rows, :])
                add = ee * part
                total = add[0:8]
                for at in range(8, add.shape[0], 8):
                    total = total + add[at:at + 8]
                hits[side, x] = hits[side, x] + total
                return part

            part = lax.fori_loop(0, n, body, start, unroll=4)
            pay[mz + rows.start:mz + rows.stop, :] = -(1.0 - rr * rr) * part
        for x in range(n):
            pay[2 * mz + x:2 * mz + x + 1, :] = a_all[x, 0:1, :]
        t_e, t_o = jnp.sum(hits[0], axis=1), jnp.sum(hits[1], axis=1)
        pay[2 * mz:2 * mz + n, :] = pay[2 * mz:2 * mz + n, :] - (t_o + t_e)
        pay[2 * mz + n:2 * mz + 2 * n, :] = t_o - t_e
        pay_t[...] = pack(pay, low, mz, n, mc)[:, 0:pay_t.shape[1]]


def front(u, v, w, u_lo, u_hi, w_lo, w_hi, owners):
    n, mz, ny = u.shape
    planes = 4
    steps = n // planes
    r, edge = mode_planes(mz, ny, owners)
    whole = lambda a: pl.BlockSpec(a.shape, lambda i: (0,) * a.ndim, pipeline_mode=pl.Buffered(1))
    here = lambda i: jnp.minimum(i, steps - 1)
    group = pl.BlockSpec((planes, mz, ny), lambda i: (here(i), 0, 0))
    tables = folded_tables(ny, owners, 0.5) + split_np(slab_table(mz)) + (r, edge)
    prev = pl.BlockSpec((1, mz, ny), lambda i: (jnp.maximum(here(i) * planes - 1, 0), 0, 0))
    after = pl.BlockSpec((1, mz, ny), lambda i: (jnp.minimum(i * planes + planes, n - 1), 0, 0))
    rows = width_of(mz, n)
    return pl.pallas_call(
        functools.partial(front_kernel, planes, steps, ny // owners),
        grid=(steps + 2,),
        in_specs=[whole(u_lo), whole(u_hi), prev, group, after, group, group, whole(w_lo), whole(w_hi)] + [whole(t) for t in tables],
        out_specs=[pl.BlockSpec((planes, mz, ny), lambda i: (jnp.maximum(i - 2, 0), 0, 0)),
                   pl.BlockSpec((ny, rows), lambda i: (0, 0), pipeline_mode=pl.Buffered(1))],
        out_shape=[jax.ShapeDtypeStruct((n, mz, ny), jnp.float32), jax.ShapeDtypeStruct((ny, rows), jnp.bfloat16)],
        scratch_shapes=[pltpu.VMEM((n, mz, ny), jnp.float32), pltpu.VMEM((mz, ny), jnp.float32),
                        pltpu.VMEM((2, planes * mz, ny), jnp.bfloat16), pltpu.VMEM((2, planes * mz, ny), jnp.bfloat16),
                        pltpu.VMEM((planes * mz, ny), jnp.float32), pltpu.VMEM((planes * mz, ny), jnp.float32),
                        pltpu.VMEM((2, n, 8, ny), jnp.float32), pltpu.VMEM((round_up(rows), ny), jnp.float32),
                        pltpu.VMEM((3 * piece_of(mz, n), ny), jnp.float32), pltpu.VMEM((2, n, ny), jnp.float32)],
        compiler_params=pltpu.CompilerParams(dimension_semantics=("arbitrary",), vmem_limit_bytes=VMEM_LIMIT),
        name="front",
    )(u_lo, u_hi, u, u, u, v, w, w_lo, w_hi, *tables)


def owner_kernel(ngx, ngz, n, recv, r, rn, wrap, gain, edge, first, last, inv, xh, xl, jh, jl,
                 out, buf, hits, mixed, res, low):
    mz, lanes = r.shape
    half = mz // 2
    mc = lanes // (ngx * ngz)
    step = ngz * mc
    unpack(buf, low, recv, mz, n, mc)
    hits[...] = jnp.zeros_like(hits)

    def carries(up, down, rows):
        power = rn[rows, :]
        reach = 1
        while reach < ngx:
            up = up + power * pltpu.roll(up, step * reach, 1)
            down = down + power * pltpu.roll(down, lanes - step * reach, 1)
            reach *= 2
            if reach < ngx:
                power = power * power
        close = wrap[rows, :]
        return close * pltpu.roll(up, step, 1), close * pltpu.roll(down, lanes - step, 1)

    def fold(value):
        total = value[0:8]
        for at in range(8, value.shape[0], 8):
            total = total + value[at:at + 8]
        return total

    def below(rows):
        return slice(mz + rows.start, mz + rows.stop)

    for rows in chunks(mz, 16):
        up, down = carries(buf[rows, :], buf[below(rows), :], rows)
        res[rows, :] = gain[rows, :] * r[rows, :] * up
        res[below(rows), :] = gain[rows, :] * down
    for rows in chunks(mz, 32):
        rr = r[rows, :]
        side = 0 if rows.start < half else 1

        def rise(x, value):
            hits[0, side, x] = hits[0, side, x] + fold(value)
            return rr * value

        def fall(k, value):
            hits[1, side, n - 1 - k] = hits[1, side, n - 1 - k] + fold(value)
            return rr * value

        lax.fori_loop(0, n, rise, res[rows, :], unroll=True)
        lax.fori_loop(0, n, fall, res[below(rows), :], unroll=True)

    def beside(field, before):
        if ngz == 1:
            return field
        if before:
            return jnp.where(first[...] > 0.0, pltpu.roll(field, lanes - mc * (ngz - 1), 1), pltpu.roll(field, mc, 1))
        return jnp.where(last[...] > 0.0, pltpu.roll(field, mc * (ngz - 1), 1), pltpu.roll(field, lanes - mc, 1))

    t_e = jnp.sum(hits[0, 0] + hits[1, 0], axis=1)
    t_o = jnp.sum(hits[0, 1] + hits[1, 1], axis=1)
    own = buf[2 * mz:2 * mz + n, :] - (t_o + t_e)
    rhs = own - beside(buf[2 * mz + n:2 * mz + 2 * n, :] + (t_o - t_e), True)
    line = jnp.concatenate([rhs[:, d * step:(d + 1) * step] for d in range(ngx)], axis=0)
    across = (jh[...], jl[...])
    table = (xh[...], xl[...])
    line = dot3(split(line), across)
    line = dot3(table, split(line)) * inv[...]
    line = dot3(table, split(line))
    line = dot3(split(line), across)
    g = jnp.concatenate([line[d * n:(d + 1) * n] for d in range(ngx)], axis=1)
    g_next = beside(g, False)
    mixed[0] = g - g_next
    mixed[1] = g + g_next
    res[2 * mz:2 * mz + n, :] = g
    res[2 * mz + n:2 * mz + 2 * n, :] = g_next
    for rows in chunks(mz, 32):
        rr = r[rows, :]
        side = 0 if rows.start < half else 1
        zero = jnp.zeros_like(rr)
        up = lax.fori_loop(0, n, lambda x, t: rr * t + mixed[side, pl.ds(x, 1), :], zero, unroll=True)
        buf[rows, :] = buf[rows, :] - edge[rows, :] * up
        down = lax.fori_loop(0, n, lambda k, t: rr * (t + mixed[side, pl.ds(n - 1 - k, 1), :]), zero, unroll=True)
        buf[below(rows), :] = buf[below(rows), :] - edge[rows, :] * down
    for rows in chunks(mz, 16):
        up, down = carries(buf[rows, :], buf[below(rows), :], rows)
        res[rows, :] = up
        res[below(rows), :] = down
    res[0:1, :] = pltpu.roll(g[n - 1:n], step, 1)
    res[mz:mz + 1, :] = pltpu.roll(g[0:1], lanes - step, 1)
    out[...] = pack(res, low, mz, n, mc)[:, 0:out.shape[1]]


def owner_tables(ngx, ngz, n, mz, ny):
    nx, ndev = ngx * n, ngx * ngz
    mc = ny // ndev
    start = (lax.axis_index("gx") * ngz + lax.axis_index("gz")) * mc
    order = slab_order(mz)
    wall = lax.dynamic_slice_in_dim(jnp.asarray(wall_part(ny, ndev), jnp.float32), start, mc)
    across = jnp.asarray(np.sin(np.pi * order / (2 * mz)) ** 2, jnp.float32)[:, None]
    real = jnp.asarray(order > 0, jnp.float32)[:, None]
    s = jnp.sqrt(wall + across)
    theta = 2.0 * jnp.log1p(s + s * s / (1.0 + jnp.sqrt(1.0 + s * s)))
    wide = lambda t: jnp.tile(t * real, (1, ndev))
    one = jnp.exp(-theta)
    edge = jnp.asarray(slab_table(mz)[:, 1:2], jnp.float32)
    r, rn = wide(one), wide(jnp.exp(-float(n) * theta))
    wrap = wide(1.0 / (1.0 - jnp.exp(-float(nx) * theta)))
    gain = wide(-edge * one / (1.0 - one * one))
    s2 = wall + jnp.asarray(np.sin(np.pi * np.arange(nx) / nx) ** 2, jnp.float32)[:, None]
    sq, root = jnp.sqrt(s2), jnp.sqrt(1.0 + s2)
    decay = jnp.exp(-2.0 * mz * jnp.log1p(sq + s2 / (1.0 + root)))
    inv = []
    for j in range(ngz):
        bend = 1.0 + decay * decay - 2.0 * math.cos(2.0 * math.pi * j / ngz) * decay
        inv.append(-(1.0 - decay * decay) / (4.0 * float(nx * ngz) * sq * root * bend))
    slab = np.arange(ny) // mc % ngz
    first = jnp.asarray((slab == 0)[None], jnp.float32)
    last = jnp.asarray((slab == ngz - 1)[None], jnp.float32)
    edge = mode_planes(mz, ny, ndev)[1]
    sides = split_np(hartley_table(nx)) + split_np(np.kron(hartley_table(ngz), np.eye(mc)))
    return (r, rn, wrap, gain, edge, first, last, jnp.concatenate(inv, axis=1)) + sides


def owner(recv, tables, ngx, ngz, n, mz):
    ny, width = recv.shape
    return pl.pallas_call(
        functools.partial(owner_kernel, ngx, ngz, n),
        out_shape=jax.ShapeDtypeStruct((ny, width), jnp.bfloat16),
        scratch_shapes=[pltpu.VMEM((round_up(width), ny), jnp.float32), pltpu.VMEM((2, 2, n, 8, ny), jnp.float32),
                        pltpu.VMEM((2, n, ny), jnp.float32), pltpu.VMEM((round_up(width), ny), jnp.float32),
                        pltpu.VMEM((3 * piece_of(mz, n), ny), jnp.float32)],
        compiler_params=pltpu.CompilerParams(vmem_limit_bytes=VMEM_LIMIT),
        name="owner",
    )(recv, *tables)


def back_kernel(n, mc, a_hbm, ret, u, v, w, eh, el, oh, ol, th, tl, r, edge, stiff,
                p_out, u_out, v_out, w_out, a_all, now, xa, xb, pa, pb, rt, low, rims, modes, sems):
    s = pl.program_id(0)
    mz, ny = now.shape
    half = mz // 2
    tall = mz + EXTRA
    last = n // 2
    f = lambda a: a.astype(jnp.float32)
    line = lambda x: rims[pl.ds(x + 2, 1), :]
    line_next = lambda x: rt[pl.ds(2 * mz + n + jnp.clip(x, 0, n - 1), 1), :]

    def sweep():
        copies = [pltpu.make_async_copy(a_hbm.at[x], a_all.at[x + 1], sems.at[x]) for x in range(n)]
        for copy in copies:
            copy.start()
        unpack(rt, low, ret, mz, n, mc)
        rims[...] = jnp.zeros_like(rims)
        rims[1:2, :] = rt[0:1, :]
        rims[2:2 + n, :] = rt[2 * mz:2 * mz + n, :]
        rims[2 + n:3 + n, :] = rt[mz:mz + 1, :]
        now[...] = rt[0:mz, :]
        a_all[0] = rt[0:mz, :]

        def body(x, carry):
            pltpu.make_async_copy(a_hbm.at[x], a_all.at[x + 1], sems.at[x]).wait()
            here, there = line(x), line_next(x)
            for rows in chunks(mz):
                mix = here - there if rows.start < half else here + there
                new = r[rows, :] * now[rows, :] - edge[rows, :] * mix
                now[rows, :] = new
                a_all[x + 1, rows, :] = a_all[x + 1, rows, :] + new
            return carry

        lax.fori_loop(0, n, body, 0)
        for rows in chunks(mz):
            rr = r[rows, :]
            b_in = rt[mz + rows.start:mz + rows.stop, :]
            now[rows, :] = -(rr * rr * a_all[n, rows, :] + b_in) / (1.0 - rr * rr)

    def along_z(dst, begin):
        for t in range(2):
            x = n - 2 * s - t
            if not (begin and t == 0):
                now[...] = r[...] * (now[...] - a_all[x + 1])
            now[0:1, :] = line(x)
            hat = split(now[...])
            now[0:1, :] = jnp.zeros((1, ny), jnp.float32)
            both = dot(jnp.concatenate([th[...], tl[...]], axis=0), hat[0])
            pz = both[:mz] + (both[mz:] + dot(th[...], hat[1]))
            high, rest = split(pz)
            base = t * tall
            dst[0, base:base + mz, :] = high
            dst[1, base:base + mz, :] = rest
            under = (a_all[jnp.minimum(x + 1, n), 0:1, :] - pz[1:2, :] - line(x + 1) - line(x - 1)
                     + stiff[...] * line(x))
            at = lax.broadcasted_iota(jnp.int32, (EXTRA, ny), 0)
            extra = jnp.where(at == 0, line_next(x), jnp.where(at == EXTRA - 1, under, 0.0))
            high, rest = split(extra)
            dst[0, base + mz:base + tall, :] = high
            dst[1, base + mz:base + tall, :] = rest

    def along_y(src, dst):
        fold_dot(src, (eh, el, oh, ol), modes)
        for t in range(2):
            rows = slice(t * tall, (t + 1) * tall)
            even, odd = modes[rows, :ny // 2], modes[rows, ny // 2:]
            dst[t, :, :ny // 2] = even + odd
            dst[t, :, ny // 2:] = flip(even - odd)

    def finish(old, new):
        trio = ((1, old[0, :mz], old[1], new[0, :mz]), (0, old[1, :mz], new[0], new[1, :mz]))
        for k, after, full, before in trio:
            mid = full[:mz]
            p_out[k] = mid
            u_out[k] = f(u[k]) - 0.5 * (after - before)
            v_out[k] = f(v[k]) - 0.5 * wall_gap(mid)
            up, down = pltpu.roll(full, tall - 1, 0)[:mz], pltpu.roll(full, 1, 0)[:mz]
            w_out[k] = f(w[k]) - 0.5 * (up - down)

    xs, ps = (xa, xb), (pa, pb)

    @pl.when(s == 0)
    def _():
        sweep()
        along_z(xa, True)

    @pl.when(s == 1)
    def _():
        along_y(xa, pa)
        along_z(xb, False)

    for par in range(2):
        @pl.when((s >= 2) & (s <= last) & (lax.rem(s, 2) == par))
        def _():
            along_y(xs[1 - par], ps[1 - par])
            along_z(xs[par], False)
            finish(ps[par], ps[1 - par])

    @pl.when(s == last + 1)
    def _():
        along_y(xs[last % 2], ps[last % 2])
        finish(ps[1 - last % 2], ps[last % 2])


def back(a_loc, ret, u, v, w, owners):
    n, mz, ny = u.shape
    r, edge = mode_planes(mz, ny, owners)
    stiff = jnp.asarray(4.0 + 4.0 * wall_part(ny, owners)[None], jnp.float32)
    tables = tuple(t.T for t in folded_tables(ny, owners, 1.0)) + split_np(slab_table(mz).T) + (r, edge, stiff)
    whole = lambda a: pl.BlockSpec(a.shape, lambda i: (0,) * a.ndim, pipeline_mode=pl.Buffered(1))
    pair = pl.BlockSpec((2, mz, ny), lambda s: (jnp.clip(n // 2 + 1 - s, 0, n // 2 - 1), 0, 0))
    shape = jax.ShapeDtypeStruct((n, mz, ny), jnp.float32)
    tall = mz + EXTRA
    return pl.pallas_call(
        functools.partial(back_kernel, n, ny // owners),
        grid=(n // 2 + 2,),
        in_specs=[pl.BlockSpec(memory_space=pl.ANY), whole(ret)] + [pair] * 3 + [whole(t) for t in tables],
        out_specs=[pair] * 4,
        out_shape=[shape] * 4,
        scratch_shapes=[pltpu.VMEM((n + 1, mz, ny), jnp.float32), pltpu.VMEM((mz, ny), jnp.float32),
                        pltpu.VMEM((2, 2 * tall, ny), jnp.bfloat16), pltpu.VMEM((2, 2 * tall, ny), jnp.bfloat16),
                        pltpu.VMEM((2, tall, ny), jnp.float32), pltpu.VMEM((2, tall, ny), jnp.float32),
                        pltpu.VMEM((round_up(ret.shape[1]), ny), jnp.float32),
                        pltpu.VMEM((3 * piece_of(mz, n), ny), jnp.float32), pltpu.VMEM((n + 8, ny), jnp.float32),
                        pltpu.VMEM((2 * tall, ny), jnp.float32), pltpu.SemaphoreType.DMA((n,))],
        compiler_params=pltpu.CompilerParams(dimension_semantics=("arbitrary",), vmem_limit_bytes=VMEM_LIMIT),
        name="back",
    )(a_loc, ret, u, v, w, *tables)


def on_device(u, v, w):
    n, mz, ny = u.shape
    ngx, ngz = lax.axis_size("gx"), lax.axis_size("gz")
    ndev = ngx * ngz
    tables = owner_tables(ngx, ngz, n, mz, ny)
    w_lo, w_hi = shift_pair(w[:, 0], w[:, -1], "gz")
    u_lo, u_hi = shift_pair(u[:1], u[-1:], "gx")
    a_loc, pay = front(u, v, w, u_lo, u_hi, w_lo, w_hi, ndev)

    def swap(message):
        parts = message.reshape(ndev, ny // ndev, -1)
        return lax.all_to_all(parts, ("gx", "gz"), 0, 0).reshape(ny, -1)

    ret = swap(owner(swap(pay), tables, ngx, ngz, n, mz))
    return back(a_loc, ret, u, v, w, ndev)


def solution(mesh):
    spec = P("gx", "gz", None)
    return jax.shard_map(on_device, mesh=mesh, in_specs=(spec,) * 3, out_specs=(spec,) * 4, check_vma=False)
```

```python
import functools
import math
import ml_dtypes
import numpy as np
import jax
import jax.numpy as jnp
from jax import lax
from jax.experimental import pallas as pl
from jax.experimental.pallas import tpu as pltpu
from jax.sharding import PartitionSpec as P

HI = lax.Precision.HIGHEST


def slab_order(count):
    return np.concatenate([np.arange(0, count, 2), np.arange(1, count, 2)])


def slab_table(count):
    order = slab_order(count)
    cell = np.arange(count)
    table = math.sqrt(2.0 / count) * np.sin(np.pi * np.outer(order, cell) / count)
    table[0, 0] = 1.0
    return table


def sine_table(count):
    index = np.arange(1, count + 1)
    angle = np.outer(index, index) % (2 * (count + 1)) * (np.pi / (count + 1))
    return math.sqrt(2.0 / (count + 1)) * np.sin(angle)


def hartley_table(count):
    index = np.arange(count)
    angle = np.outer(index, index) % count * (2.0 * np.pi / count)
    return np.cos(angle) + np.sin(angle)


def wall_order(count, owners):
    places, each, third = np.arange(count // 2), count // owners, count // owners // 3
    owner, slot = places // each, places % each
    low = owner * third + slot
    high = count // 6 + owner * 2 * third + slot - third
    rank = np.where(slot < third, low, high)
    return np.concatenate([2 * rank, 2 * rank + 1])


def wall_part(count, owners):
    return np.sin((wall_order(count, owners) + 1) * (np.pi / (2 * count + 2))) ** 2


def folded_tables(count, owners, scale):
    table = scale * sine_table(count)[:count // 2, wall_order(count, owners)]
    return split_np(table[:, :count // 2]) + split_np(table[:, count // 2:])


def shift_pair(first, last, axis):
    count = lax.axis_size(axis)
    forward = [(i, (i + 1) % count) for i in range(count)]
    backward = [(target, source) for source, target in forward]
    return lax.ppermute(last, axis, forward), lax.ppermute(first, axis, backward)


VMEM_LIMIT = 60 * 1024 * 1024
EXTRA = 16


def split_np(table):
    wide = np.asarray(table, np.float32)
    high = wide.astype(ml_dtypes.bfloat16)
    low = (np.asarray(table, np.float64) - high.astype(np.float64)).astype(ml_dtypes.bfloat16)
    return jnp.asarray(high), jnp.asarray(low)


def split(value):
    high = value.astype(jnp.bfloat16)
    return high, (value - high.astype(jnp.float32)).astype(jnp.bfloat16)


def dot(a, b):
    return jnp.dot(a, b, preferred_element_type=jnp.float32)


def dot3(a, b):
    return dot(a[0], b[0]) + (dot(a[1], b[0]) + dot(a[0], b[1]))


def mode_planes(m_cells, ny, owners):
    order = slab_order(m_cells)
    s = np.sqrt(np.sin(np.pi * order / (2 * m_cells))[:, None] ** 2 + wall_part(ny, owners)[None])
    r = (np.sqrt(1 + s * s) - s) ** 2 * (order > 0)[:, None]
    edge = slab_table(m_cells)[:, 1] * (order > 0)
    edge = np.broadcast_to(edge[:, None], r.shape)
    return jnp.asarray(r, jnp.float32), jnp.asarray(edge, jnp.float32)


def round_up(count, unit=128):
    return -(-count // unit) * unit


def spans(mz, n):
    half, third = mz // 2, mz // 6
    return [(2 * mz, 2 * n), (0, third), (half, third), (mz, third), (mz + half, third)]


def piece_of(mz, n):
    return -(-sum(size for _, size in spans(mz, n)) // 24) * 8


def width_of(mz, n):
    return 2 * mz + 2 * n + piece_of(mz, n)


def slot_third(shape, mc):
    lane = lax.broadcasted_iota(jnp.int32, shape, 1)
    return lax.div(lax.rem(lane, mc), mc // 3)


def pack(rows, low, mz, n, mc):
    at, main, piece = 0, 2 * mz + 2 * n, piece_of(mz, n)
    lanes = rows.shape[1]
    low[...] = jnp.zeros_like(low)
    for start, size in spans(mz, n):
        value = rows[start:start + size, :]
        low[at:at + size, :] = value - value.astype(jnp.bfloat16).astype(jnp.float32)
        at += size
    third = slot_third((piece, lanes), mc)
    mix = jnp.where(third == 1, pltpu.roll(low[piece:2 * piece, :], mc // 3, 1), low[0:piece, :])
    mix = jnp.where(third == 2, pltpu.roll(low[2 * piece:3 * piece, :], mc // 3 * 2, 1), mix)
    rows[main:main + piece, :] = mix
    return rows[...].T.astype(jnp.bfloat16)


def unpack(rows, low, message, mz, n, mc):
    at, main, piece = 0, 2 * mz + 2 * n, piece_of(mz, n)
    lanes = rows.shape[1]
    rows[0:message.shape[1], :] = message[...].astype(jnp.float32).T
    first = slot_third((piece, lanes), mc) == 0
    mix = rows[main:main + piece, :]
    for k in range(3):
        moved = pltpu.roll(mix, lanes - k * (mc // 3), 1) if k else mix
        low[k * piece:(k + 1) * piece, :] = jnp.where(first, moved, 0.0)
    for start, size in spans(mz, n):
        rows[start:start + size, :] = rows[start:start + size, :] + low[at:at + size, :]
        at += size


def chunks(rows, size=24):
    half = rows // 2
    size = math.gcd(size, half)
    return [slice(i, i + size) for i in range(0, rows, size)]


def flip(field):
    rows, width = field.shape
    if width % 128:
        return jnp.flip(field, 1)
    at = 127 - lax.broadcasted_iota(jnp.int32, (rows, 128), 1)
    parts = [jnp.take_along_axis(field[:, k:k + 128], at, axis=1) for k in range(0, width, 128)]
    return jnp.concatenate(parts[::-1], axis=1)


def fold_dot(src, tables, out):
    middle = out.shape[1] // 2
    for k, (high, low) in enumerate((tables[:2], tables[2:])):
        cols = slice(k * middle, (k + 1) * middle)
        lhs = jnp.concatenate([src[0, :, cols], src[1, :, cols], src[0, :, cols]], axis=1)
        out[:, cols] = dot(lhs, jnp.concatenate([high[...], high[...], low[...]], axis=0))


def wall_gap(field):
    ny = field.shape[1]
    at = lax.broadcasted_iota(jnp.int32, field.shape, 1)
    after = jnp.where(at == ny - 1, 0.0, pltpu.roll(field, ny - 1, 1))
    before = jnp.where(at == 0, 0.0, pltpu.roll(field, 1, 1))
    return after - before


def front_kernel(planes, steps, mc, u_lo, u_hi, u_prev, u, u_next, v, w, w_lo, w_hi, eh, el, oh, ol, th, tl, r, edge,
                 a_out, pay_t, a_all, now, xa, xb, sa, sb, hits, pay, low, rims):
    i = pl.program_id(0)
    mz, ny = now.shape
    n = planes * steps
    half = mz // 2
    f = lambda t: t.astype(jnp.float32)

    def diverge(dst):
        row = lax.broadcasted_iota(jnp.int32, (mz, ny), 0)
        for p in range(planes):
            if p == 0:
                before = jnp.where(i == 0, f(u_lo[0]), f(u_prev[0]))
            else:
                before = f(u[p - 1])
            if p == planes - 1:
                after = jnp.where(i == steps - 1, f(u_hi[0]), f(u_next[0]))
            else:
                after = f(u[p + 1])
            mid = f(w[p])
            w_after = jnp.where(row == mz - 1, rims[1, pl.ds(i * planes + p, 1), :], pltpu.roll(mid, mz - 1, 0))
            w_before = jnp.where(row == 0, rims[0, pl.ds(i * planes + p, 1), :], pltpu.roll(mid, 1, 0))
            div = (after - before) + (w_after - w_before) + wall_gap(f(v[p]))
            left, right = div[:, :ny // 2], flip(div[:, ny // 2:])
            for cols, value in ((slice(0, ny // 2), left + right), (slice(ny // 2, ny), left - right)):
                high, rest = split(value)
                dst[0, p * mz:(p + 1) * mz, cols] = high
                dst[1, p * mz:(p + 1) * mz, cols] = rest

    def along_y(src, dst):
        fold_dot(src, (eh, el, oh, ol), dst)

    def along_z(src):
        for p in range(planes):
            part = split(src[p * mz:(p + 1) * mz, :])
            right = jnp.concatenate([part[0], part[1], part[0]], axis=0)
            left = jnp.concatenate([th[...], th[...], tl[...]], axis=1)
            a = r[...] * now[...] + dot(left, right)
            now[...] = a
            a_out[p] = a
            a_all[(i - 2) * planes + p] = a

    xs, ss = (xa, xb), (sa, sb)

    @pl.when(i == 0)
    def _():
        now[...] = jnp.zeros_like(now)
        rims[0] = f(w_lo[1])
        rims[1] = f(w_hi[0])
        diverge(xa)

    @pl.when(i == 1)
    def _():
        along_y(xa, sa)
        diverge(xb)

    for par in range(2):
        @pl.when((i >= 2) & (i < steps) & (lax.rem(i, 2) == par))
        def _():
            along_y(xs[1 - par], ss[1 - par])
            diverge(xs[par])
            along_z(ss[par])

    @pl.when(i == steps)
    def _():
        along_y(xs[(steps - 1) % 2], ss[(steps - 1) % 2])
        along_z(ss[steps % 2])

    @pl.when(i == steps + 1)
    def _():
        along_z(ss[(steps + 1) % 2])
        pay[0:mz, :] = now[...]
        hits[...] = jnp.zeros_like(hits)
        for rows in chunks(mz, 16):
            rr = r[rows, :]
            ee = edge[rows, :]
            side = 0 if rows.start < half else 1
            start = -(rr * rr / (1.0 - rr * rr)) * now[rows, :]

            def body(k, part):
                x = n - 1 - k
                part = rr * (part - a_all[x, rows, :])
                add = ee * part
                total = add[0:8]
                for at in range(8, add.shape[0], 8):
                    total = total + add[at:at + 8]
                hits[side, x] = hits[side, x] + total
                return part

            part = lax.fori_loop(0, n, body, start, unroll=4)
            pay[mz + rows.start:mz + rows.stop, :] = -(1.0 - rr * rr) * part
        for x in range(n):
            pay[2 * mz + x:2 * mz + x + 1, :] = a_all[x, 0:1, :]
        t_e, t_o = jnp.sum(hits[0], axis=1), jnp.sum(hits[1], axis=1)
        pay[2 * mz:2 * mz + n, :] = pay[2 * mz:2 * mz + n, :] - (t_o + t_e)
        pay[2 * mz + n:2 * mz + 2 * n, :] = t_o - t_e
        pay_t[...] = pack(pay, low, mz, n, mc)[:, 0:pay_t.shape[1]]


def front(u, v, w, u_lo, u_hi, w_lo, w_hi, owners):
    n, mz, ny = u.shape
    planes = 2
    steps = n // planes
    r, edge = mode_planes(mz, ny, owners)
    whole = lambda a: pl.BlockSpec(a.shape, lambda i: (0,) * a.ndim, pipeline_mode=pl.Buffered(1))
    here = lambda i: jnp.minimum(i, steps - 1)
    group = pl.BlockSpec((planes, mz, ny), lambda i: (here(i), 0, 0))
    tables = folded_tables(ny, owners, 0.5) + split_np(slab_table(mz)) + (r, edge)
    prev = pl.BlockSpec((1, mz, ny), lambda i: (jnp.maximum(here(i) * planes - 1, 0), 0, 0))
    after = pl.BlockSpec((1, mz, ny), lambda i: (jnp.minimum(i * planes + planes, n - 1), 0, 0))
    rows = width_of(mz, n)
    return pl.pallas_call(
        functools.partial(front_kernel, planes, steps, ny // owners),
        grid=(steps + 2,),
        in_specs=[whole(u_lo), whole(u_hi), prev, group, after, group, group, whole(w_lo), whole(w_hi)] + [whole(t) for t in tables],
        out_specs=[pl.BlockSpec((planes, mz, ny), lambda i: (jnp.maximum(i - 2, 0), 0, 0)),
                   pl.BlockSpec((ny, rows), lambda i: (0, 0), pipeline_mode=pl.Buffered(1))],
        out_shape=[jax.ShapeDtypeStruct((n, mz, ny), jnp.float32), jax.ShapeDtypeStruct((ny, rows), jnp.bfloat16)],
        scratch_shapes=[pltpu.VMEM((n, mz, ny), jnp.float32), pltpu.VMEM((mz, ny), jnp.float32),
                        pltpu.VMEM((2, planes * mz, ny), jnp.bfloat16), pltpu.VMEM((2, planes * mz, ny), jnp.bfloat16),
                        pltpu.VMEM((planes * mz, ny), jnp.float32), pltpu.VMEM((planes * mz, ny), jnp.float32),
                        pltpu.VMEM((2, n, 8, ny), jnp.float32), pltpu.VMEM((round_up(rows), ny), jnp.float32),
                        pltpu.VMEM((3 * piece_of(mz, n), ny), jnp.float32), pltpu.VMEM((2, n, ny), jnp.float32)],
        compiler_params=pltpu.CompilerParams(dimension_semantics=("arbitrary",), vmem_limit_bytes=VMEM_LIMIT),
        name="front",
    )(u_lo, u_hi, u, u, u, v, w, w_lo, w_hi, *tables)


def owner_kernel(ngx, ngz, n, recv, r, rn, wrap, gain, edge, first, last, inv, xh, xl, jh, jl,
                 out, buf, hits, mixed, res, low):
    mz, lanes = r.shape
    half = mz // 2
    mc = lanes // (ngx * ngz)
    step = ngz * mc
    unpack(buf, low, recv, mz, n, mc)
    hits[...] = jnp.zeros_like(hits)

    def carries(up, down, rows):
        power = rn[rows, :]
        reach = 1
        while reach < ngx:
            up = up + power * pltpu.roll(up, step * reach, 1)
            down = down + power * pltpu.roll(down, lanes - step * reach, 1)
            reach *= 2
            if reach < ngx:
                power = power * power
        close = wrap[rows, :]
        return close * pltpu.roll(up, step, 1), close * pltpu.roll(down, lanes - step, 1)

    def fold(value):
        total = value[0:8]
        for at in range(8, value.shape[0], 8):
            total = total + value[at:at + 8]
        return total

    def below(rows):
        return slice(mz + rows.start, mz + rows.stop)

    for rows in chunks(mz, 16):
        up, down = carries(buf[rows, :], buf[below(rows), :], rows)
        res[rows, :] = gain[rows, :] * r[rows, :] * up
        res[below(rows), :] = gain[rows, :] * down
    for rows in chunks(mz, 32):
        rr = r[rows, :]
        side = 0 if rows.start < half else 1

        def rise(x, value):
            hits[0, side, x] = hits[0, side, x] + fold(value)
            return rr * value

        def fall(k, value):
            hits[1, side, n - 1 - k] = hits[1, side, n - 1 - k] + fold(value)
            return rr * value

        lax.fori_loop(0, n, rise, res[rows, :], unroll=True)
        lax.fori_loop(0, n, fall, res[below(rows), :], unroll=True)

    def beside(field, before):
        if ngz == 1:
            return field
        if before:
            return jnp.where(first[...] > 0.0, pltpu.roll(field, lanes - mc * (ngz - 1), 1), pltpu.roll(field, mc, 1))
        return jnp.where(last[...] > 0.0, pltpu.roll(field, mc * (ngz - 1), 1), pltpu.roll(field, lanes - mc, 1))

    t_e = jnp.sum(hits[0, 0] + hits[1, 0], axis=1)
    t_o = jnp.sum(hits[0, 1] + hits[1, 1], axis=1)
    own = buf[2 * mz:2 * mz + n, :] - (t_o + t_e)
    rhs = own - beside(buf[2 * mz + n:2 * mz + 2 * n, :] + (t_o - t_e), True)
    line = jnp.concatenate([rhs[:, d * step:(d + 1) * step] for d in range(ngx)], axis=0)
    across = (jh[...], jl[...])
    table = (xh[...], xl[...])
    line = dot3(split(line), across)
    line = dot3(table, split(line)) * inv[...]
    line = dot3(table, split(line))
    line = dot3(split(line), across)
    g = jnp.concatenate([line[d * n:(d + 1) * n] for d in range(ngx)], axis=1)
    g_next = beside(g, False)
    mixed[0] = g - g_next
    mixed[1] = g + g_next
    res[2 * mz:2 * mz + n, :] = g
    res[2 * mz + n:2 * mz + 2 * n, :] = g_next
    for rows in chunks(mz, 32):
        rr = r[rows, :]
        side = 0 if rows.start < half else 1
        zero = jnp.zeros_like(rr)
        up = lax.fori_loop(0, n, lambda x, t: rr * t + mixed[side, pl.ds(x, 1), :], zero, unroll=True)
        buf[rows, :] = buf[rows, :] - edge[rows, :] * up
        down = lax.fori_loop(0, n, lambda k, t: rr * (t + mixed[side, pl.ds(n - 1 - k, 1), :]), zero, unroll=True)
        buf[below(rows), :] = buf[below(rows), :] - edge[rows, :] * down
    for rows in chunks(mz, 16):
        up, down = carries(buf[rows, :], buf[below(rows), :], rows)
        res[rows, :] = up
        res[below(rows), :] = down
    res[0:1, :] = pltpu.roll(g[n - 1:n], step, 1)
    res[mz:mz + 1, :] = pltpu.roll(g[0:1], lanes - step, 1)
    out[...] = pack(res, low, mz, n, mc)[:, 0:out.shape[1]]


def owner_tables(ngx, ngz, n, mz, ny):
    nx, ndev = ngx * n, ngx * ngz
    mc = ny // ndev
    start = (lax.axis_index("gx") * ngz + lax.axis_index("gz")) * mc
    order = slab_order(mz)
    wall = lax.dynamic_slice_in_dim(jnp.asarray(wall_part(ny, ndev), jnp.float32), start, mc)
    across = jnp.asarray(np.sin(np.pi * order / (2 * mz)) ** 2, jnp.float32)[:, None]
    real = jnp.asarray(order > 0, jnp.float32)[:, None]
    s = jnp.sqrt(wall + across)
    theta = 2.0 * jnp.log1p(s + s * s / (1.0 + jnp.sqrt(1.0 + s * s)))
    wide = lambda t: jnp.tile(t * real, (1, ndev))
    one = jnp.exp(-theta)
    edge = jnp.asarray(slab_table(mz)[:, 1:2], jnp.float32)
    r, rn = wide(one), wide(jnp.exp(-float(n) * theta))
    wrap = wide(1.0 / (1.0 - jnp.exp(-float(nx) * theta)))
    gain = wide(-edge * one / (1.0 - one * one))
    s2 = wall + jnp.asarray(np.sin(np.pi * np.arange(nx) / nx) ** 2, jnp.float32)[:, None]
    sq, root = jnp.sqrt(s2), jnp.sqrt(1.0 + s2)
    decay = jnp.exp(-2.0 * mz * jnp.log1p(sq + s2 / (1.0 + root)))
    inv = []
    for j in range(ngz):
        bend = 1.0 + decay * decay - 2.0 * math.cos(2.0 * math.pi * j / ngz) * decay
        inv.append(-(1.0 - decay * decay) / (4.0 * float(nx * ngz) * sq * root * bend))
    slab = np.arange(ny) // mc % ngz
    first = jnp.asarray((slab == 0)[None], jnp.float32)
    last = jnp.asarray((slab == ngz - 1)[None], jnp.float32)
    edge = mode_planes(mz, ny, ndev)[1]
    sides = split_np(hartley_table(nx)) + split_np(np.kron(hartley_table(ngz), np.eye(mc)))
    return (r, rn, wrap, gain, edge, first, last, jnp.concatenate(inv, axis=1)) + sides


def owner(recv, tables, ngx, ngz, n, mz):
    ny, width = recv.shape
    return pl.pallas_call(
        functools.partial(owner_kernel, ngx, ngz, n),
        out_shape=jax.ShapeDtypeStruct((ny, width), jnp.bfloat16),
        scratch_shapes=[pltpu.VMEM((round_up(width), ny), jnp.float32), pltpu.VMEM((2, 2, n, 8, ny), jnp.float32),
                        pltpu.VMEM((2, n, ny), jnp.float32), pltpu.VMEM((round_up(width), ny), jnp.float32),
                        pltpu.VMEM((3 * piece_of(mz, n), ny), jnp.float32)],
        compiler_params=pltpu.CompilerParams(vmem_limit_bytes=VMEM_LIMIT),
        name="owner",
    )(recv, *tables)


def back_kernel(n, mc, a_hbm, ret, u, v, w, eh, el, oh, ol, th, tl, r, edge, stiff,
                p_out, u_out, v_out, w_out, a_all, now, xa, xb, pa, pb, rt, low, rims, modes, sems):
    s = pl.program_id(0)
    mz, ny = now.shape
    half = mz // 2
    tall = mz + EXTRA
    last = n // 2
    f = lambda a: a.astype(jnp.float32)
    line = lambda x: rims[pl.ds(x + 2, 1), :]
    line_next = lambda x: rt[pl.ds(2 * mz + n + jnp.clip(x, 0, n - 1), 1), :]

    def sweep():
        copies = [pltpu.make_async_copy(a_hbm.at[x], a_all.at[x + 1], sems.at[x]) for x in range(n)]
        for copy in copies:
            copy.start()
        unpack(rt, low, ret, mz, n, mc)
        rims[...] = jnp.zeros_like(rims)
        rims[1:2, :] = rt[0:1, :]
        rims[2:2 + n, :] = rt[2 * mz:2 * mz + n, :]
        rims[2 + n:3 + n, :] = rt[mz:mz + 1, :]
        now[...] = rt[0:mz, :]
        a_all[0] = rt[0:mz, :]

        def body(x, carry):
            pltpu.make_async_copy(a_hbm.at[x], a_all.at[x + 1], sems.at[x]).wait()
            here, there = line(x), line_next(x)
            for rows in chunks(mz):
                mix = here - there if rows.start < half else here + there
                new = r[rows, :] * now[rows, :] - edge[rows, :] * mix
                now[rows, :] = new
                a_all[x + 1, rows, :] = a_all[x + 1, rows, :] + new
            return carry

        lax.fori_loop(0, n, body, 0)
        for rows in chunks(mz):
            rr = r[rows, :]
            b_in = rt[mz + rows.start:mz + rows.stop, :]
            now[rows, :] = -(rr * rr * a_all[n, rows, :] + b_in) / (1.0 - rr * rr)

    def along_z(dst, begin):
        for t in range(2):
            x = n - 2 * s - t
            if not (begin and t == 0):
                now[...] = r[...] * (now[...] - a_all[x + 1])
            now[0:1, :] = line(x)
            hat = split(now[...])
            now[0:1, :] = jnp.zeros((1, ny), jnp.float32)
            both = dot(jnp.concatenate([th[...], tl[...]], axis=0), hat[0])
            pz = both[:mz] + (both[mz:] + dot(th[...], hat[1]))
            high, rest = split(pz)
            base = t * tall
            dst[0, base:base + mz, :] = high
            dst[1, base:base + mz, :] = rest
            under = (a_all[jnp.minimum(x + 1, n), 0:1, :] - pz[1:2, :] - line(x + 1) - line(x - 1)
                     + stiff[...] * line(x))
            at = lax.broadcasted_iota(jnp.int32, (EXTRA, ny), 0)
            extra = jnp.where(at == 0, line_next(x), jnp.where(at == EXTRA - 1, under, 0.0))
            high, rest = split(extra)
            dst[0, base + mz:base + tall, :] = high
            dst[1, base + mz:base + tall, :] = rest

    def along_y(src, dst):
        fold_dot(src, (eh, el, oh, ol), modes)
        for t in range(2):
            rows = slice(t * tall, (t + 1) * tall)
            even, odd = modes[rows, :ny // 2], modes[rows, ny // 2:]
            dst[t, :, :ny // 2] = even + odd
            dst[t, :, ny // 2:] = flip(even - odd)

    def finish(old, new):
        trio = ((1, old[0, :mz], old[1], new[0, :mz]), (0, old[1, :mz], new[0], new[1, :mz]))
        for k, after, full, before in trio:
            mid = full[:mz]
            p_out[k] = mid
            u_out[k] = f(u[k]) - 0.5 * (after - before)
            v_out[k] = f(v[k]) - 0.5 * wall_gap(mid)
            up, down = pltpu.roll(full, tall - 1, 0)[:mz], pltpu.roll(full, 1, 0)[:mz]
            w_out[k] = f(w[k]) - 0.5 * (up - down)

    xs, ps = (xa, xb), (pa, pb)

    @pl.when(s == 0)
    def _():
        sweep()
        along_z(xa, True)

    @pl.when(s == 1)
    def _():
        along_y(xa, pa)
        along_z(xb, False)

    for par in range(2):
        @pl.when((s >= 2) & (s <= last) & (lax.rem(s, 2) == par))
        def _():
            along_y(xs[1 - par], ps[1 - par])
            along_z(xs[par], False)
            finish(ps[par], ps[1 - par])

    @pl.when(s == last + 1)
    def _():
        along_y(xs[last % 2], ps[last % 2])
        finish(ps[1 - last % 2], ps[last % 2])


def back(a_loc, ret, u, v, w, owners):
    n, mz, ny = u.shape
    r, edge = mode_planes(mz, ny, owners)
    stiff = jnp.asarray(4.0 + 4.0 * wall_part(ny, owners)[None], jnp.float32)
    tables = tuple(t.T for t in folded_tables(ny, owners, 1.0)) + split_np(slab_table(mz).T) + (r, edge, stiff)
    whole = lambda a: pl.BlockSpec(a.shape, lambda i: (0,) * a.ndim, pipeline_mode=pl.Buffered(1))
    pair = pl.BlockSpec((2, mz, ny), lambda s: (jnp.clip(n // 2 + 1 - s, 0, n // 2 - 1), 0, 0))
    shape = jax.ShapeDtypeStruct((n, mz, ny), jnp.float32)
    tall = mz + EXTRA
    return pl.pallas_call(
        functools.partial(back_kernel, n, ny // owners),
        grid=(n // 2 + 2,),
        in_specs=[pl.BlockSpec(memory_space=pl.ANY), whole(ret)] + [pair] * 3 + [whole(t) for t in tables],
        out_specs=[pair] * 4,
        out_shape=[shape] * 4,
        scratch_shapes=[pltpu.VMEM((n + 1, mz, ny), jnp.float32), pltpu.VMEM((mz, ny), jnp.float32),
                        pltpu.VMEM((2, 2 * tall, ny), jnp.bfloat16), pltpu.VMEM((2, 2 * tall, ny), jnp.bfloat16),
                        pltpu.VMEM((2, tall, ny), jnp.float32), pltpu.VMEM((2, tall, ny), jnp.float32),
                        pltpu.VMEM((round_up(ret.shape[1]), ny), jnp.float32),
                        pltpu.VMEM((3 * piece_of(mz, n), ny), jnp.float32), pltpu.VMEM((n + 8, ny), jnp.float32),
                        pltpu.VMEM((2 * tall, ny), jnp.float32), pltpu.SemaphoreType.DMA((n,))],
        compiler_params=pltpu.CompilerParams(dimension_semantics=("arbitrary",), vmem_limit_bytes=VMEM_LIMIT),
        name="back",
    )(a_loc, ret, u, v, w, *tables)


def on_device(u, v, w):
    n, mz, ny = u.shape
    ngx, ngz = lax.axis_size("gx"), lax.axis_size("gz")
    ndev = ngx * ngz
    tables = owner_tables(ngx, ngz, n, mz, ny)
    ends = jnp.stack([w[:, 0], w[:, -1]])
    w_lo, w_hi = shift_pair(ends, ends, "gz")
    u_lo, u_hi = shift_pair(u[:1], u[-1:], "gx")
    a_loc, pay = front(u, v, w, u_lo, u_hi, w_lo, w_hi, ndev)

    def swap(message):
        parts = message.reshape(ndev, ny // ndev, -1)
        return lax.all_to_all(parts, ("gx", "gz"), 0, 0).reshape(ny, -1)

    ret = swap(owner(swap(pay), tables, ngx, ngz, n, mz))
    return back(a_loc, ret, u, v, w, ndev)


def solution(mesh):
    spec = P("gx", "gz", None)
    return jax.shard_map(on_device, mesh=mesh, in_specs=(spec,) * 3, out_specs=(spec,) * 4, check_vma=False)
```
